32 devices in a mesh: dp: 8 (over z, x), tensor: 4 (over y, core).
Axes of the slice: x: 2, y: 2, z: 4, core: 2. Of those that a mesh axis runs over, the one named last changes fastest.
Arguments:
- gate_act: bfloat16 [1024, 26624], P('dp', 'tensor'), may hold values from -8 to 8
- up_act: bfloat16 [1024, 26624], P('dp', 'tensor'), may hold values from -6 to 6
- down_codes: bfloat16 [26624, 16384], P('tensor', 'dp'), may hold values from -4 to 4
- down_scales: float32 [208, 128], P('tensor', 'dp'), may hold values from 0.0024514517 to 0.024514517
- grad_out: bfloat16 [1024, 16384], P('tensor', 'dp'), may hold values from -6 to 6
Outputs:
- layer_output: bfloat16 [1024, 16384], P('tensor', 'dp')
- gate_grad: bfloat16 [1024, 26624], P('dp', 'tensor')
- up_grad: bfloat16 [1024, 26624], P('dp', 'tensor')
The draws below stay inside these ranges and needn't reach their ends.
All inputs are finite; a program needn't handle non-finite values.
Results may differ from the reference program's by a relative error of at most 0.027.
Values may be sent and summed in bfloat16 or wider, within the bound.
No kernel may reach another device: no remote copies, remote signals or barrier semaphores. Data moves between devices by JAX's collectives and lax.ppermute only.
A program may use at most 192 MiB of HBM per device.

```python
import math
import jax
import jax.numpy as jnp
from jax import lax

D = 16384
FF = 26624
BLOCK = 128
TOKENS = 1024
FL = 6656
DL = 2048


def raised(result, stream_key, source, target, blocks, factor):
    owner, partner = [(jnp.arange(result.shape[position]) // (result.shape[position] // blocks)).reshape([-1 if axis == position else 1 for axis in range(result.ndim)]) for position in (source, target)]
    chosen = jax.random.permutation(stream_key, blocks)[partner]
    strong = (owner == chosen) | (owner == (partner + blocks // 2) % blocks)
    return jnp.where(strong, factor * result, result)


def steps_of(own_key, shape, cuts, least, high):
    def one(position, blocks):
        heights = jax.random.uniform(jax.random.fold_in(jax.random.fold_in(own_key, 6), position), (blocks,), jnp.float32, least / len(cuts), high / len(cuts))
        return jnp.repeat(jnp.exp(heights), shape[position] // blocks).reshape((-1,) + (1,) * (len(shape) - position - 1))

    level = one(*cuts[0])
    for cut in cuts[1:]:
        level = level * one(*cut)
    return level


def gaussian(stream_key, shape, deviation, limit, cuts=(), kind=jnp.bfloat16):
    values = deviation * jax.random.normal(stream_key, shape, jnp.float32)
    if cuts:
        values = values * steps_of(stream_key, shape, cuts, -0.22, 0.18)
    return jnp.clip(values, -limit, limit).astype(kind)


def noise_with(rng, dims, deviation, most, pieces, heavy, kind=jnp.bfloat16):
    result = deviation * jax.random.normal(rng, dims, jnp.float32)
    if pieces:
        result = result * steps_of(rng, dims, pieces, -0.22, 0.18)
    return jnp.clip(raised(result, jax.random.fold_in(rng, 3), *heavy), -most, most).astype(kind)


def setup_inputs(seed: int = 0) -> dict:
    splits = jax.random.split(jax.random.key(seed), 6)
    return {
        "gate_act": gaussian(splits[0], (TOKENS, FF), 2.0, 8.0, ((0, 8), (1, 4))),
        "up_act": gaussian(splits[1], (TOKENS, FF), 1.0, 6.0, ((0, 8), (1, 4))),
        "down_codes": gaussian(splits[2], (FF, D), 1.0, 4.0, ((0, 4), (1, 8))),
        "down_scales": jnp.clip(jnp.exp(math.log(0.024514517) - 2.3025851 * jax.random.uniform(splits[3], (FF // BLOCK, D // BLOCK), jnp.float32) ** steps_of(splits[3], (FF // BLOCK, D // BLOCK), ((0, 4), (1, 8)), -0.2, 0.2)), 0.0024514517, 0.024514517),
        "grad_out": noise_with(splits[4], (TOKENS, D), 1.0, 6.0, ((0, 4), (1, 8)), (1, 0, 8, 2.0)),
    }


def sylvester(matrix_order):
    indices = jnp.arange(matrix_order, dtype=jnp.int32)
    common_bits = indices[:, None] & indices[None, :]
    parity = jnp.zeros((matrix_order, matrix_order), jnp.int32)
    for section_bit in range(max(matrix_order.bit_length() - 1, 0)):
        parity = parity + (common_bits >> section_bit & 1)
    return (1 - 2 * (parity % 2)).astype(jnp.float32)

def dequantize(code_block, scale_block):
    row_count, col_count = code_block.shape
    expanded = code_block.astype(jnp.float32).reshape(row_count // BLOCK, BLOCK, col_count // BLOCK, BLOCK)
    return (expanded * scale_block[:, None, :, None]).reshape(row_count, col_count).astype(jnp.bfloat16)

def rotate(values):
    row_count = values.shape[0]
    groups = FF // FL
    shaped = values.astype(jnp.float32).reshape(row_count, groups, FL // BLOCK, BLOCK)
    mixed_values = jnp.einsum('rgbc,hg,dc->rhbd', shaped, sylvester(groups), sylvester(BLOCK), precision=lax.Precision.HIGHEST)
    return (mixed_values / math.sqrt(groups * BLOCK)).reshape(row_count, FF).astype(jnp.bfloat16)

def reference(gate_act, up_act, down_codes, down_scales, grad_out):
    gate_wide = gate_act.astype(jnp.float32)
    up_wide = up_act.astype(jnp.float32)
    sigmoid_gate = jax.nn.sigmoid(gate_wide)
    silu_gate = gate_wide * sigmoid_gate
    hidden = (silu_gate * up_wide).astype(jnp.bfloat16)
    rotated = rotate(hidden)
    groups = FF // FL
    rot_groups = jnp.moveaxis(rotated.reshape(TOKENS, groups, FL), 1, 0)
    code_groups = down_codes.reshape(groups, FL, D)
    scale_groups = down_scales.reshape(groups, FL // BLOCK, D // BLOCK)

    def forward_step(running, inputs):
        rot_part, code_part, scale_part = inputs
        group_term = jnp.dot(rot_part, dequantize(code_part, scale_part), preferred_element_type=jnp.float32)
        group_term = lax.optimization_barrier(group_term.astype(jnp.bfloat16))
        return (running + group_term.astype(jnp.float32), None)
    running, unused = lax.scan(forward_step, jnp.zeros((TOKENS, D), jnp.float32), (rot_groups, code_groups, scale_groups))
    layer_output = running.astype(jnp.bfloat16)
    col_groups = D // DL
    grad_groups = jnp.moveaxis(grad_out.reshape(TOKENS, col_groups, DL), 1, 0)
    code_cols = jnp.moveaxis(down_codes.reshape(FF, col_groups, DL), 1, 0)
    scale_cols = jnp.moveaxis(down_scales.reshape(FF // BLOCK, col_groups, DL // BLOCK), 1, 0)

    def backward_step(running, inputs):
        grad_part, code_part, scale_part = inputs
        weight = dequantize(code_part, scale_part)
        group_term = lax.dot_general(grad_part, weight, (((1,), (1,)), ((), ())), preferred_element_type=jnp.float32)
        group_term = lax.optimization_barrier(group_term.astype(jnp.bfloat16))
        return (running + group_term.astype(jnp.float32), None)
    running, unused = lax.scan(backward_step, jnp.zeros((TOKENS, FF), jnp.float32), (grad_groups, code_cols, scale_cols))
    grad_rotated = running.astype(jnp.bfloat16)
    grad_hidden = rotate(grad_rotated).astype(jnp.float32)
    up_grad = (grad_hidden * silu_gate).astype(jnp.bfloat16)
    gate_grad = (grad_hidden * up_wide * sigmoid_gate * (1.0 + gate_wide * (1.0 - sigmoid_gate))).astype(jnp.bfloat16)
    return (layer_output, gate_grad, up_grad)
```

```python
import math

import jax
import jax.numpy as jnp
import numpy as np
from jax import lax
from jax.experimental import pallas as pl
from jax.experimental.pallas import tpu as pltpu
from jax.sharding import PartitionSpec as P

BLOCK = 128
STREAMS = 4
VMEM_LIMIT = 40 * 1024 * 1024
F32, BF16 = jnp.float32, jnp.bfloat16


def after(value, *earlier):
    return lax.optimization_barrier((value, *earlier))[0]


def sylvester(order):
    matrix = np.ones((1, 1), np.float32)
    while matrix.shape[0] < order:
        matrix = np.block([[matrix, matrix], [matrix, -matrix]])
    return matrix


def ring_cycle(count):
    return [*range(0, count, 2), *reversed(range(1, count, 2))]


def ring_tables(count):
    cycle = ring_cycle(count)
    place = np.argsort(cycle)
    behind = [[cycle[(place[i] - r) % count] for r in range(count)] for i in range(count)]
    ahead = [[(place[j] - place[i]) % count for j in range(count)] for i in range(count)]
    return np.concatenate([behind, ahead], axis=1).astype(np.int32)


def params():
    return pltpu.CompilerParams(vmem_limit_bytes=VMEM_LIMIT)


def spec_smem():
    return pl.BlockSpec(memory_space=pltpu.SMEM)


def dequantize_into(weight_ref, codes_ref, scales_ref, row0, col0):
    for i in range(codes_ref.shape[0] // BLOCK):
        for j in range(codes_ref.shape[1] // BLOCK):
            at = (pl.ds(i * BLOCK, BLOCK), pl.ds(j * BLOCK, BLOCK))
            wide = codes_ref[at].astype(F32) * scales_ref[row0 + i, col0 + j]
            weight_ref[at] = wide.astype(BF16)


def mixed(values, mix, scale):
    high = values.astype(BF16)
    low = (values - high.astype(F32)).astype(BF16)
    total = jnp.dot(high, mix, preferred_element_type=F32) + jnp.dot(
        low, mix, preferred_element_type=F32
    )
    return (total * scale).astype(BF16)


def mix_kernel(scale, sign_ref, mix_ref, own_ref, other_ref, out_ref):
    for j in range(own_ref.shape[1] // BLOCK):
        at = (slice(None), pl.ds(j * BLOCK, BLOCK))
        values = own_ref[at].astype(F32) * sign_ref[0] + other_ref[at].astype(F32)
        out_ref[at] = mixed(values, mix_ref[...], scale)


def local_mix(own, other, sign, mix, scale):
    rows, cols = own.shape
    return pl.pallas_call(
        lambda *refs: mix_kernel(scale, *refs),
        out_shape=jax.ShapeDtypeStruct((rows, cols), BF16),
        in_specs=[spec_smem()] + [pl.BlockSpec(memory_space=pltpu.VMEM)] * 3,
        out_specs=pl.BlockSpec(memory_space=pltpu.VMEM),
        compiler_params=params(),
        cost_estimate=pl.CostEstimate(
            flops=4 * rows * cols * BLOCK, bytes_accessed=6 * rows * cols, transcendentals=0
        ),
        name="local_mix",
    )(sign, mix, own, other)


def grads_kernel(scale, tile, sign_ref, mix_ref, own_ref, other_ref, gate_ref, up_ref, *refs):
    gate_grad_ref, up_grad_ref = refs[-2:]
    for j in range(tile // BLOCK):
        at = (slice(None), pl.ds(j * BLOCK, BLOCK))
        values = own_ref[at].astype(F32) * sign_ref[0] + other_ref[at].astype(F32)
        grad = mixed(values, mix_ref[...], scale).astype(F32)
        gate = gate_ref[at].astype(F32)
        sigmoid = jax.nn.sigmoid(gate)
        up_grad_ref[at] = (grad * (gate * sigmoid)).astype(BF16)
        gate_grad_ref[at] = (
            grad * up_ref[at].astype(F32) * sigmoid * (1.0 + gate * (1.0 - sigmoid))
        ).astype(BF16)


def local_grads(own, other, sign, mix, scale, gate_act, up_act, start, tile, made):
    rows, cols = own.shape
    whole = pl.BlockSpec((rows, tile), lambda i: (0, start // tile + i))
    part = pl.BlockSpec((rows, tile), lambda i: (0, i))
    rest = [pl.BlockSpec(memory_space=pl.ANY)] * len(made)
    return pl.pallas_call(
        lambda *refs: grads_kernel(scale, tile, *refs),
        grid=(cols // tile,),
        out_shape=[jax.ShapeDtypeStruct(gate_act.shape, BF16)] * 2,
        in_specs=[
            spec_smem(),
            pl.BlockSpec((BLOCK, BLOCK), lambda i: (0, 0)),
            part,
            part,
            whole,
            whole,
            *rest,
        ],
        out_specs=[whole, whole],
        input_output_aliases={6 + k: k for k in range(len(made))},
        compiler_params=params(),
        cost_estimate=pl.CostEstimate(
            flops=4 * rows * cols * BLOCK,
            bytes_accessed=12 * rows * cols,
            transcendentals=rows * cols,
        ),
        name="local_grads",
    )(sign, mix, own, other, gate_act, up_act, *made)


def arrange_kernel(count, group_ref, table_ref, *refs):
    out_ref = refs[-1]
    rows = out_ref.shape[0] // count
    for offset, block in enumerate(refs[:-1]):
        per = block.shape[0] // rows
        for i in range(per):
            place = table_ref[count + (group_ref[0] ^ offset) * per + i]
            start = pl.multiple_of(place * rows, rows)
            out_ref[pl.ds(start, rows), :] = block[pl.ds(i * rows, rows), :]


def arrange_rows(held, group, table):
    blocks = [held[offset] for offset in range(len(held))]
    rows, cols = blocks[0].shape
    return pl.pallas_call(
        lambda *refs: arrange_kernel(table.shape[0] // 2, *refs),
        out_shape=jax.ShapeDtypeStruct((rows * len(blocks), cols), BF16),
        in_specs=[spec_smem()] * 2 + [pl.BlockSpec(memory_space=pltpu.VMEM)] * len(blocks),
        out_specs=pl.BlockSpec(memory_space=pltpu.VMEM),
        compiler_params=params(),
        cost_estimate=pl.CostEstimate(
            flops=0, bytes_accessed=4 * rows * cols * len(blocks), transcendentals=0
        ),
        name="arrange_rows",
    )(group, table, *blocks)


def backward_kernel(row_block, scales_ref, grad_ref, codes_ref, out_ref, weight_ref):
    row0 = row_block + pl.program_id(0) * (codes_ref.shape[0] // BLOCK)
    dequantize_into(weight_ref, codes_ref, scales_ref, row0, 0)
    out_ref[...] = lax.dot_general(
        grad_ref[...], weight_ref[...], (((1,), (1,)), ((), ())), preferred_element_type=F32
    ).astype(BF16)


def backward_product(grad_rows, codes, scales, start, cols, tile):
    tokens, depth = grad_rows.shape
    return pl.pallas_call(
        lambda *refs: backward_kernel(start // BLOCK, *refs),
        grid=(cols // tile,),
        out_shape=pltpu.HBM((tokens, cols), BF16),
        in_specs=[
            spec_smem(),
            pl.BlockSpec((tokens, depth), lambda i: (0, 0)),
            pl.BlockSpec((tile, depth), lambda i: (start // tile + i, 0)),
        ],
        out_specs=pl.BlockSpec((tokens, tile), lambda i: (0, i)),
        scratch_shapes=[pltpu.VMEM((tile, depth), BF16)],
        compiler_params=params(),
        cost_estimate=pl.CostEstimate(
            flops=2 * tokens * depth * cols,
            bytes_accessed=2 * (tokens * depth + depth * cols + tokens * cols),
            transcendentals=0,
        ),
        name="backward_product",
    )(scales, grad_rows, codes)


def forward_kernel(count, row_block, has_sum, order_ref, scales_ref, *refs):
    blocks, codes_ref = refs[:count], refs[count]
    sum_ref = refs[count + 1] if has_sum else None
    out_ref, rows_ref, weight_ref = refs[-3:]
    tile = codes_ref.shape[1]

    @pl.when(pl.program_id(0) == 0)
    def _():
        for r, block in enumerate(blocks):
            size = block.shape[0]
            rows_ref[pl.ds(pl.multiple_of(order_ref[r] * size, size), size), :] = block[...]

    dequantize_into(
        weight_ref, codes_ref, scales_ref, row_block, pl.program_id(0) * (tile // BLOCK)
    )
    total = jnp.dot(rows_ref[...], weight_ref[...], preferred_element_type=F32)
    if has_sum:
        total = total + sum_ref[...]
    out_ref[...] = total.astype(out_ref.dtype)


def forward_product(blocks, order, codes, scales, start, running, out_dtype):
    size, cols = blocks[0].shape
    tokens, width = size * len(blocks), codes.shape[1]
    tile = min(256, width)
    sums = [] if running is None else [running]
    sliced = pl.BlockSpec((tokens, tile), lambda i: (0, i))
    return pl.pallas_call(
        lambda *refs: forward_kernel(len(blocks), start // BLOCK, bool(sums), *refs),
        grid=(width // tile,),
        out_shape=pltpu.HBM((tokens, width), out_dtype),
        in_specs=[
            spec_smem(),
            spec_smem(),
            *[pl.BlockSpec((size, cols), lambda i: (0, 0))] * len(blocks),
            pl.BlockSpec((pl.Element(cols), pl.Element(tile)), lambda i: (start, i * tile)),
            *[sliced] * len(sums),
        ],
        out_specs=sliced,
        scratch_shapes=[pltpu.VMEM((tokens, cols), BF16), pltpu.VMEM((cols, tile), BF16)],
        compiler_params=params(),
        cost_estimate=pl.CostEstimate(
            flops=2 * tokens * cols * width,
            bytes_accessed=2 * (tokens * cols + cols * width) + 8 * tokens * width,
            transcendentals=0,
        ),
        name="forward_product",
    )(order, scales, *blocks, codes, *sums)


def stream_columns(total, tile):
    units = total // tile
    count = min(STREAMS, units)
    sizes = sorted((units + k) // count for k in range(count))
    starts = np.cumsum([0, *sizes[:-1]])
    return [(int(a) * tile, int(b) * tile) for a, b in zip(starts, sizes)]


def on_device(gate_act, up_act, down_codes, down_scales, grad_out):
    groups, ring = lax.axis_size("tensor"), lax.axis_size("dp")
    group, member = lax.axis_index("tensor"), lax.axis_index("dp")
    bits = list(reversed(range(groups.bit_length() - 1)))
    rows, hidden_units = gate_act.shape
    tile = 256 if hidden_units % 256 == 0 else BLOCK
    streams = stream_columns(hidden_units, tile)
    cycle = ring_cycle(ring)
    half = ring // 2
    table = lax.dynamic_index_in_dim(jnp.asarray(ring_tables(ring)), member, 0, keepdims=False)

    pairs = {
        step: [(cycle[i], cycle[(i + step) % ring]) for i in range(ring)] for step in (1, -1)
    }

    def partner(value, bit):
        return lax.ppermute(value, "tensor", [(i, i ^ 1 << bit) for i in range(groups)])

    def sign(bit):
        return jnp.where(group >> bit & 1 == 1, -1.0, 1.0).astype(F32)

    def paired(own, other, bit):
        return (own.astype(F32) * sign(bit) + other.astype(F32)).astype(BF16)

    last_sign = sign(bits[-1]).reshape(1)
    mix = jnp.asarray(sylvester(BLOCK), BF16)
    scale = 1.0 / math.sqrt(groups * BLOCK)

    def reach(k, step):
        return half if (k % 2 == 0) == (step == 1) else ring - 1 - half

    def hidden(start, size):
        gate = lax.slice_in_dim(gate_act, start, start + size, axis=1).astype(F32)
        up = lax.slice_in_dim(up_act, start, start + size, axis=1).astype(F32)
        return (gate * jax.nn.sigmoid(gate) * up).astype(BF16)

    def gathered():
        held = {0: after(grad_out, token)}
        for bit in bits:
            held.update({o ^ 1 << bit: partner(value, bit) for o, value in list(held.items())})
            if bit == bits[0]:
                arrived = held[1 << bit]
        return held, arrived

    rotated = []
    token = None
    for k, (start, size) in enumerate(streams):
        if k == len(streams) // 2:
            held, token = gathered()
        own = hidden(start, size)
        if token is not None:
            own = after(own, token)
        other = token = partner(own, bits[0])
        for previous, bit in zip(bits, bits[1:]):
            own = paired(own, other, previous)
            other = partner(own, bit)
        rotated.append(local_mix(own, other, last_sign, mix, scale))
    grad_rows = arrange_rows(held, group.astype(jnp.int32).reshape(1), table)

    running = None
    for k, (start, size) in enumerate(streams):
        blocks = [rotated[k]] + [None] * (ring - 1)
        for step in (1, -1):
            moving = rotated[k]
            for hop in range(1, reach(k, step) + 1):
                moving = lax.ppermute(moving, "dp", pairs[step])
                blocks[hop * step % ring] = moving
        running = forward_product(
            blocks,
            table,
            down_codes,
            down_scales,
            start,
            running,
            BF16 if k == len(streams) - 1 else F32,
        )
    layer_output = lax.psum_scatter(running, "tensor", scatter_dimension=0, tiled=True)

    grads = []
    for k, (start, size) in enumerate(streams):
        partial = backward_product(grad_rows, down_codes, down_scales, start, size, tile)

        def term(offset):
            at = offset % ring * rows
            return lax.slice_in_dim(partial, at, at + rows, axis=0)

        total = term(0).astype(F32)
        for step in (1, -1):
            far = reach(k, step)
            moving = term(step * far)
            for hop in range(far - 1, -1, -1):
                moving = lax.ppermute(moving, "dp", pairs[step])
                if hop:
                    moving = (moving.astype(F32) + term(step * hop).astype(F32)).astype(BF16)
            total = total + moving.astype(F32)
        own = total.astype(BF16)
        other = partner(own, bits[0])
        for previous, bit in zip(bits, bits[1:]):
            own = paired(own, other, previous)
            other = partner(own, bit)
        grads = local_grads(
            own, other, last_sign, mix, scale, gate_act, up_act, start, tile, grads
        )
    gate_grad, up_grad = grads
    return (layer_output, gate_grad, up_grad)


def solution(mesh):
    return jax.shard_map(
        on_device,
        mesh=mesh,
        in_specs=(
            P("dp", "tensor"),
            P("dp", "tensor"),
            P("tensor", "dp"),
            P("tensor", "dp"),
            P("tensor", "dp"),
        ),
        out_specs=(P("tensor", "dp"), P("dp", "tensor"), P("dp", "tensor")),
        check_vma=False,
    )
```

```python
import math

import jax
import jax.numpy as jnp
import numpy as np
from jax import lax
from jax.experimental import pallas as pl
from jax.experimental.pallas import tpu as pltpu
from jax.sharding import PartitionSpec as P

BLOCK = 128
SMALL_SHARE = 4 / 26
VMEM_LIMIT = 40 * 1024 * 1024
F32, BF16 = jnp.float32, jnp.bfloat16


def after(value, *earlier):
    return lax.optimization_barrier((value, *earlier))[0]


def sylvester(order):
    matrix = np.ones((1, 1), np.float32)
    while matrix.shape[0] < order:
        matrix = np.block([[matrix, matrix], [matrix, -matrix]])
    return matrix


def ring_cycle(count):
    return [*range(0, count, 2), *reversed(range(1, count, 2))]


def ring_tables(count):
    cycle = ring_cycle(count)
    place = np.argsort(cycle)
    behind = [[cycle[(place[i] - r) % count] for r in range(count)] for i in range(count)]
    ahead = [[(place[j] - place[i]) % count for j in range(count)] for i in range(count)]
    return np.concatenate([behind, ahead], axis=1).astype(np.int32)


def params():
    return pltpu.CompilerParams(vmem_limit_bytes=VMEM_LIMIT)


def spec_smem():
    return pl.BlockSpec(memory_space=pltpu.SMEM)


def dequantize_into(weight_ref, codes_ref, scales_ref, row0, col0):
    for i in range(codes_ref.shape[0] // BLOCK):
        for j in range(codes_ref.shape[1] // BLOCK):
            at = (pl.ds(i * BLOCK, BLOCK), pl.ds(j * BLOCK, BLOCK))
            wide = codes_ref[at].astype(F32) * scales_ref[row0 + i, col0 + j]
            weight_ref[at] = wide.astype(BF16)


def mixed(values, mix, scale):
    high = values.astype(BF16)
    low = (values - high.astype(F32)).astype(BF16)
    total = jnp.dot(high, mix, preferred_element_type=F32) + jnp.dot(
        low, mix, preferred_element_type=F32
    )
    return (total * scale).astype(BF16)


def mix_kernel(scale, sign_ref, mix_ref, own_ref, other_ref, out_ref):
    for j in range(own_ref.shape[1] // BLOCK):
        at = (slice(None), pl.ds(j * BLOCK, BLOCK))
        values = own_ref[at].astype(F32) * sign_ref[0] + other_ref[at].astype(F32)
        out_ref[at] = mixed(values, mix_ref[...], scale)


def local_mix(own, other, sign, mix, scale):
    rows, cols = own.shape
    return pl.pallas_call(
        lambda *refs: mix_kernel(scale, *refs),
        out_shape=jax.ShapeDtypeStruct((rows, cols), BF16),
        in_specs=[spec_smem()] + [pl.BlockSpec(memory_space=pltpu.VMEM)] * 3,
        out_specs=pl.BlockSpec(memory_space=pltpu.VMEM),
        compiler_params=params(),
        cost_estimate=pl.CostEstimate(
            flops=4 * rows * cols * BLOCK, bytes_accessed=6 * rows * cols, transcendentals=0
        ),
        name="local_mix",
    )(sign, mix, own, other)


def grads_kernel(scale, tile, sign_ref, mix_ref, own_ref, other_ref, gate_ref, up_ref, *refs):
    gate_grad_ref, up_grad_ref = refs[-2:]
    for j in range(tile // BLOCK):
        at = (slice(None), pl.ds(j * BLOCK, BLOCK))
        values = own_ref[at].astype(F32) * sign_ref[0] + other_ref[at].astype(F32)
        grad = mixed(values, mix_ref[...], scale).astype(F32)
        gate = gate_ref[at].astype(F32)
        sigmoid = jax.nn.sigmoid(gate)
        up_grad_ref[at] = (grad * (gate * sigmoid)).astype(BF16)
        gate_grad_ref[at] = (
            grad * up_ref[at].astype(F32) * sigmoid * (1.0 + gate * (1.0 - sigmoid))
        ).astype(BF16)


def local_grads(own, other, sign, mix, scale, gate_act, up_act, start, tile, made):
    rows, cols = own.shape
    whole = pl.BlockSpec((rows, tile), lambda i: (0, start // tile + i))
    part = pl.BlockSpec((rows, tile), lambda i: (0, i))
    rest = [pl.BlockSpec(memory_space=pl.ANY)] * len(made)
    return pl.pallas_call(
        lambda *refs: grads_kernel(scale, tile, *refs),
        grid=(cols // tile,),
        out_shape=[jax.ShapeDtypeStruct(gate_act.shape, BF16)] * 2,
        in_specs=[
            spec_smem(),
            pl.BlockSpec((BLOCK, BLOCK), lambda i: (0, 0)),
            part,
            part,
            whole,
            whole,
            *rest,
        ],
        out_specs=[whole, whole],
        input_output_aliases={6 + k: k for k in range(len(made))},
        compiler_params=params(),
        cost_estimate=pl.CostEstimate(
            flops=4 * rows * cols * BLOCK,
            bytes_accessed=12 * rows * cols,
            transcendentals=rows * cols,
        ),
        name="local_grads",
    )(sign, mix, own, other, gate_act, up_act, *made)


def arrange_kernel(table_ref, rows_ref, out_ref):
    count = table_ref.shape[0] // 2
    size = out_ref.shape[0] // count
    for i in range(count):
        start = pl.multiple_of(table_ref[count + i] * size, size)
        out_ref[pl.ds(start, size), :] = rows_ref[pl.ds(i * size, size), :]


def arrange_rows(rows, table):
    return pl.pallas_call(
        arrange_kernel,
        out_shape=jax.ShapeDtypeStruct(rows.shape, BF16),
        in_specs=[spec_smem(), pl.BlockSpec(memory_space=pltpu.VMEM)],
        out_specs=pl.BlockSpec(memory_space=pltpu.VMEM),
        compiler_params=params(),
        cost_estimate=pl.CostEstimate(flops=0, bytes_accessed=4 * rows.size, transcendentals=0),
        name="arrange_rows",
    )(table, rows)


def backward_kernel(row_block, scales_ref, grad_ref, codes_ref, *refs):
    out_ref, weight_ref = refs[-2:]
    row0 = row_block + pl.program_id(0) * (codes_ref.shape[0] // BLOCK)
    dequantize_into(weight_ref, codes_ref, scales_ref, row0, 0)
    out_ref[...] = lax.dot_general(
        grad_ref[...], weight_ref[...], (((1,), (1,)), ((), ())), preferred_element_type=F32
    ).astype(BF16)


def backward_product(grad_rows, codes, scales, start, cols, tile, pieces):
    tokens, depth = grad_rows.shape
    (first, count), made = pieces
    return pl.pallas_call(
        lambda *refs: backward_kernel(start // BLOCK + first * (tile // BLOCK), *refs),
        grid=(count,),
        out_shape=pltpu.HBM((tokens, cols), BF16),
        in_specs=[
            spec_smem(),
            pl.BlockSpec((tokens, depth), lambda i: (0, 0)),
            pl.BlockSpec((tile, depth), lambda i: (start // tile + first + i, 0)),
            *[pl.BlockSpec(memory_space=pl.ANY)] * len(made),
        ],
        out_specs=pl.BlockSpec((tokens, tile), lambda i: (0, first + i)),
        scratch_shapes=[pltpu.VMEM((tile, depth), BF16)],
        input_output_aliases={3 + k: k for k in range(len(made))},
        compiler_params=params(),
        cost_estimate=pl.CostEstimate(
            flops=2 * tokens * depth * count * tile,
            bytes_accessed=2 * (tokens * depth + (depth + tokens) * count * tile),
            transcendentals=0,
        ),
        name="backward_product",
    )(scales, grad_rows, codes, *made)


def forward_kernel(count, row_block, col_block, has_sum, order_ref, scales_ref, *refs):
    blocks, codes_ref = refs[:count], refs[count]
    sum_ref = refs[count + 1] if has_sum else None
    out_ref, rows_ref, weight_ref = refs[-3:]
    tile = codes_ref.shape[1]

    @pl.when(pl.program_id(0) == 0)
    def _():
        for r, block in enumerate(blocks):
            size = block.shape[0]
            rows_ref[pl.ds(pl.multiple_of(order_ref[r] * size, size), size), :] = block[...]

    col0 = col_block + pl.program_id(0) * (tile // BLOCK)
    dequantize_into(weight_ref, codes_ref, scales_ref, row_block, col0)
    total = jnp.dot(rows_ref[...], weight_ref[...], preferred_element_type=F32)
    if has_sum:
        total = total + sum_ref[...]
    out_ref[...] = total.astype(out_ref.dtype)


def forward_product(blocks, order, codes, scales, start, columns, running, offset, out_dtype):
    size, depth = blocks[0].shape
    tokens, (first, width) = size * len(blocks), columns
    tile = min(256, width)
    sums = [] if running is None else [running]
    return pl.pallas_call(
        lambda *refs: forward_kernel(
            len(blocks), start // BLOCK, first // BLOCK, bool(sums), *refs
        ),
        grid=(width // tile,),
        out_shape=pltpu.HBM((tokens, width), out_dtype),
        in_specs=[
            spec_smem(),
            spec_smem(),
            *[
                pl.BlockSpec((size, depth), lambda i: (0, 0), pipeline_mode=pl.Buffered(1))
            ] * len(blocks),
            pl.BlockSpec(
                (pl.Element(depth), pl.Element(tile)), lambda i: (start, (first // tile + i) * tile)
            ),
            *[pl.BlockSpec((tokens, tile), lambda i: (0, offset // tile + i))] * len(sums),
        ],
        out_specs=pl.BlockSpec((tokens, tile), lambda i: (0, i)),
        scratch_shapes=[pltpu.VMEM((tokens, depth), BF16), pltpu.VMEM((depth, tile), BF16)],
        compiler_params=params(),
        cost_estimate=pl.CostEstimate(
            flops=2 * tokens * depth * width,
            bytes_accessed=2 * (tokens * depth + depth * width) + 8 * tokens * width,
            transcendentals=0,
        ),
        name="forward_product",
    )(order, scales, *blocks, codes, *sums)


def stream_columns(sizes, tile):
    starts = np.cumsum([0, *sizes[:-1]])
    return [(int(a) * tile, int(b) * tile) for a, b in zip(starts, sizes)]


class Gather:
    def __init__(self, ring, first, own):
        self.ring, self.hop = ring, 0
        half = ring["count"] // 2
        self.reach = {first: half, -first: ring["count"] - 1 - half}
        self.blocks = {0: own}

    def advance(self, *tokens):
        self.hop += 1
        for step, reach in self.reach.items():
            if self.hop <= reach:
                moving = after(self.blocks[(self.hop - 1) * step % self.ring["count"]], *tokens)
                self.blocks[self.hop * step % self.ring["count"]] = self.ring["send"](moving, step)

    def arrived(self):
        return [
            self.blocks[self.hop * step % self.ring["count"]]
            for step, reach in self.reach.items()
            if self.hop <= reach
        ]

    def all_blocks(self):
        return [self.blocks[r] for r in range(self.ring["count"])]


class Scatter:
    def __init__(self, ring, first, partial):
        self.ring, self.hop, self.partial = ring, 0, partial
        half = ring["count"] // 2
        self.reach = {first: half, -first: ring["count"] - 1 - half}
        self.sums = {}

    def term(self, offset):
        rows = self.partial.shape[0] // self.ring["count"]
        at = offset % self.ring["count"] * rows
        return lax.slice_in_dim(self.partial, at, at + rows, axis=0)

    def advance(self, *tokens):
        self.hop += 1
        for step, reach in self.reach.items():
            if self.hop <= reach:
                moving = self.term(step * (reach - self.hop + 1))
                if self.hop > 1:
                    moving = (self.sums[step].astype(F32) + moving.astype(F32)).astype(BF16)
                self.sums[step] = self.ring["send"](after(moving, *tokens), step)

    def arrived(self):
        return [self.sums[step] for step, reach in self.reach.items() if self.hop <= reach]

    def total(self):
        parts = [self.term(0), *self.sums.values()]
        return sum(part.astype(F32) for part in parts).astype(BF16)


def on_device(gate_act, up_act, down_codes, down_scales, grad_out):
    groups, ring = lax.axis_size("tensor"), lax.axis_size("dp")
    group, member = lax.axis_index("tensor"), lax.axis_index("dp")
    bits = list(reversed(range(groups.bit_length() - 1)))
    rows, hidden_units = gate_act.shape
    tile = 256 if hidden_units % 256 == 0 else BLOCK
    units = hidden_units // tile
    small = max(1, round(units * SMALL_SHARE))
    large = (units - small) // 2
    ahead_streams = stream_columns([small, large, units - small - large], tile)
    back_streams = stream_columns([units - small - large, large, small], tile)
    cycle = ring_cycle(ring)
    table = lax.dynamic_index_in_dim(jnp.asarray(ring_tables(ring)), member, 0, keepdims=False)
    around = {
        "count": ring,
        "send": lambda value, step: lax.ppermute(
            value, "dp", [(cycle[i], cycle[(i + step) % ring]) for i in range(ring)]
        ),
    }

    def partner(value, bit):
        return lax.ppermute(value, "tensor", [(i, i ^ 1 << bit) for i in range(groups)])

    def sign(bit):
        return jnp.where(group >> bit & 1 == 1, -1.0, 1.0).astype(F32)

    def paired(own, other, bit):
        return (own.astype(F32) * sign(bit) + other.astype(F32)).astype(BF16)

    last_sign = sign(bits[-1]).reshape(1)
    mix = jnp.asarray(sylvester(BLOCK), BF16)
    scale = 1.0 / math.sqrt(groups * BLOCK)

    def hidden(start, size):
        gate = lax.slice_in_dim(gate_act, start, start + size, axis=1).astype(F32)
        up = lax.slice_in_dim(up_act, start, start + size, axis=1).astype(F32)
        return (gate * jax.nn.sigmoid(gate) * up).astype(BF16)

    def exchanged(own, token):
        own = after(own, *token)
        other = arrived = partner(own, bits[0])
        for previous, bit in zip(bits, bits[1:]):
            own = paired(own, other, previous)
            other = partner(own, bit)
        return own, other, arrived

    gathers, token = [], []
    for k, (start, size) in enumerate(ahead_streams):
        own, other, arrived = exchanged(hidden(start, size), token)
        token = [arrived]
        if k == 1:
            gathered = lax.all_gather(after(grad_out, arrived), "tensor", axis=0, tiled=True)
        rotated = local_mix(own, other, last_sign, mix, scale)
        gathers.append(Gather(around, 1 if k % 2 == 0 else -1, rotated))
        gathers[k].advance()
        if k:
            gathers[0].advance(*token)

    half = down_codes.shape[1] // 2
    running, whole_sum = {}, []

    def forward(k, columns, *tokens):
        start, _ = ahead_streams[k]
        first = columns[0]
        earlier = [] if k == 0 else [whole_sum[0]] if k == 1 else [running[first]]
        running[first] = forward_product(
            gathers[k].all_blocks(),
            after(table, *tokens),
            down_codes,
            down_scales,
            start,
            columns,
            earlier[0] if earlier else None,
            first if k == 1 else 0,
            BF16 if k == len(gathers) - 1 else F32,
        )
        if k == 0:
            whole_sum.append(running[first])
        return running[first]

    partials = {}

    def backward(k, piece, *tokens):
        start, cols = back_streams[k]
        tiles = cols // tile
        cut = (tiles + 1) // 2 if k < len(back_streams) - 1 else tiles
        place = (0, cut) if piece == 0 else (cut, tiles - cut)
        partials[k] = backward_product(
            after(grad_rows, *tokens),
            down_codes,
            down_scales,
            start,
            cols,
            tile,
            (place, [] if piece == 0 else [partials[k]]),
        )
        return partials[k]

    small_ring, ring_a, ring_b = gathers
    for _ in range(small_ring.hop, ring // 2):
        small_ring.advance()
    grad_rows = arrange_rows(gathered, table)

    last = ring // 2
    work = [
        lambda *t: forward(0, (0, 2 * half), *t),
        lambda *t: backward(0, 0, *t),
        lambda *t: backward(0, 1, *t),
        lambda *t: backward(1, 0, *t),
        lambda *t: backward(1, 1, *t),
        lambda *t: backward(2, 0, *t),
    ]
    done = []
    for hop in range(2, last + 1):
        for current in (ring_a, ring_b):
            arrived = current.arrived()
            current.advance(*done)
            if work:
                done = [work.pop(0)(*arrived, *done)]
    while work:
        done = [work.pop(0)(*done)]

    work = [
        lambda *t: forward(1, (0, half), *t),
        lambda *t: forward(1, (half, half), *t),
        lambda *t: forward(2, (0, half), *t),
        lambda *t: forward(2, (half, half), *t),
    ]
    sums = [Scatter(around, 1 if k % 2 == 0 else -1, partials[k]) for k in range(3)]
    sum_a, sum_b, small_sum = sums
    sum_a.advance(*ring_a.arrived())
    sum_b.advance(*ring_b.arrived())
    done = []
    for hop in range(2, last + 1):
        for current in (sum_a, sum_b):
            arrived = current.arrived()
            current.advance(*done)
            if work:
                done = [work.pop(0)(*arrived, *done)]
    while work:
        done = [work.pop(0)(*done)]
    layer_output = lax.psum_scatter(
        jnp.concatenate([running[0], running[half]], axis=1),
        "tensor",
        scatter_dimension=0,
        tiled=True,
    )
    small_sum.advance(*sum_a.arrived())
    for _ in range(last - 1):
        small_sum.advance()

    grads, token = [], []
    for k, (start, size) in enumerate(back_streams):
        own, other, arrived = exchanged(sums[k].total(), token)
        token = [arrived]
        grads = local_grads(
            own, other, last_sign, mix, scale, gate_act, up_act, start, tile, grads
        )
        if k == 0:
            token = [arrived, *grads]
    gate_grad, up_grad = grads
    return (layer_output, gate_grad, up_grad)


def solution(mesh):
    return jax.shard_map(
        on_device,
        mesh=mesh,
        in_specs=(
            P("dp", "tensor"),
            P("dp", "tensor"),
            P("tensor", "dp"),
            P("tensor", "dp"),
            P("tensor", "dp"),
        ),
        out_specs=(P("tensor", "dp"), P("dp", "tensor"), P("dp", "tensor")),
        check_vma=False,
    )
```

```python
import math

import jax
import jax.numpy as jnp
import numpy as np
from jax import lax
from jax.experimental import pallas as pl
from jax.experimental.pallas import tpu as pltpu
from jax.sharding import PartitionSpec as P

BLOCK = 128
AHEAD = (4, 11, 11)
BACK = (11, 11, 4)
VMEM_LIMIT = 40 * 1024 * 1024
F32, BF16 = jnp.float32, jnp.bfloat16


def after(value, *earlier):
    return lax.optimization_barrier((value, *earlier))[0]


def sylvester(order):
    matrix = np.ones((1, 1), np.float32)
    while matrix.shape[0] < order:
        matrix = np.block([[matrix, matrix], [matrix, -matrix]])
    return matrix


def ring_cycle(count):
    return [*range(0, count, 2), *reversed(range(1, count, 2))]


def ring_tables(count):
    cycle = ring_cycle(count)
    place = np.argsort(cycle)
    behind = [[cycle[(place[i] - r) % count] for r in range(count)] for i in range(count)]
    ahead = [[(place[j] - place[i]) % count for j in range(count)] for i in range(count)]
    return np.concatenate([behind, ahead], axis=1).astype(np.int32)


def params():
    return pltpu.CompilerParams(vmem_limit_bytes=VMEM_LIMIT)


def cost(operations, moved):
    return pl.CostEstimate(
        flops=operations // 16, bytes_accessed=moved // 16, transcendentals=0
    )


def spec_smem():
    return pl.BlockSpec(memory_space=pltpu.SMEM)


def dequantize_into(weight_ref, codes_ref, scales_ref, row0, col0):
    for i in range(codes_ref.shape[0] // BLOCK):
        for j in range(codes_ref.shape[1] // BLOCK):
            at = (pl.ds(i * BLOCK, BLOCK), pl.ds(j * BLOCK, BLOCK))
            wide = codes_ref[at].astype(F32) * scales_ref[row0 + i, col0 + j]
            weight_ref[at] = wide.astype(BF16)


def mixed(values, mix, scale):
    high = values.astype(BF16)
    low = (values - high.astype(F32)).astype(BF16)
    total = jnp.dot(high, mix, preferred_element_type=F32) + jnp.dot(
        low, mix, preferred_element_type=F32
    )
    return (total * scale).astype(BF16)


def mix_kernel(scale, sign_ref, mix_ref, own_ref, other_ref, out_ref):
    for j in range(own_ref.shape[1] // BLOCK):
        at = (slice(None), pl.ds(j * BLOCK, BLOCK))
        values = own_ref[at].astype(F32) * sign_ref[0] + other_ref[at].astype(F32)
        out_ref[at] = mixed(values, mix_ref[...], scale)


def local_mix(own, other, sign, mix, scale):
    rows, cols = own.shape
    return pl.pallas_call(
        lambda *refs: mix_kernel(scale, *refs),
        out_shape=jax.ShapeDtypeStruct((rows, cols), BF16),
        in_specs=[spec_smem()] + [pl.BlockSpec(memory_space=pltpu.VMEM)] * 3,
        out_specs=pl.BlockSpec(memory_space=pltpu.VMEM),
        compiler_params=params(),
        cost_estimate=cost(4 * rows * cols * BLOCK, 6 * rows * cols),
        name="local_mix",
    )(sign, mix, own, other)


def grads_kernel(scale, tile, sign_ref, mix_ref, own_ref, other_ref, gate_ref, up_ref, *refs):
    gate_grad_ref, up_grad_ref = refs[-2:]
    for j in range(tile // BLOCK):
        at = (slice(None), pl.ds(j * BLOCK, BLOCK))
        values = own_ref[at].astype(F32) * sign_ref[0] + other_ref[at].astype(F32)
        grad = mixed(values, mix_ref[...], scale).astype(F32)
        gate = gate_ref[at].astype(F32)
        sigmoid = jax.nn.sigmoid(gate)
        up_grad_ref[at] = (grad * (gate * sigmoid)).astype(BF16)
        gate_grad_ref[at] = (
            grad * up_ref[at].astype(F32) * sigmoid * (1.0 + gate * (1.0 - sigmoid))
        ).astype(BF16)


def local_grads(own, other, sign, mix, scale, gate_act, up_act, start, made):
    rows, cols = own.shape
    tile = math.gcd(start, cols)
    if tile % (2 * BLOCK) == 0:
        tile //= 2
    whole = pl.BlockSpec((rows, tile), lambda i: (0, start // tile + i))
    part = pl.BlockSpec((rows, tile), lambda i: (0, i))
    rest = [pl.BlockSpec(memory_space=pl.ANY)] * len(made)
    return pl.pallas_call(
        lambda *refs: grads_kernel(scale, tile, *refs),
        grid=(cols // tile,),
        out_shape=[jax.ShapeDtypeStruct(gate_act.shape, BF16)] * 2,
        in_specs=[
            spec_smem(),
            pl.BlockSpec((BLOCK, BLOCK), lambda i: (0, 0)),
            part,
            part,
            whole,
            whole,
            *rest,
        ],
        out_specs=[whole, whole],
        input_output_aliases={6 + k: k for k in range(len(made))},
        compiler_params=params(),
        cost_estimate=cost(4 * rows * cols * BLOCK, 12 * rows * cols),
        name="local_grads",
    )(sign, mix, own, other, gate_act, up_act, *made)


def arrange_kernel(count, group_ref, table_ref, *refs):
    out_ref = refs[-1]
    rows = out_ref.shape[0] // count
    for offset, block in enumerate(refs[:-1]):
        per = block.shape[0] // rows
        for i in range(per):
            place = table_ref[count + (group_ref[0] ^ offset) * per + i]
            start = pl.multiple_of(place * rows, rows)
            out_ref[pl.ds(start, rows), :] = block[pl.ds(i * rows, rows), :]


def arrange_rows(held, group, table):
    blocks = [held[offset] for offset in range(len(held))]
    rows, cols = blocks[0].shape
    return pl.pallas_call(
        lambda *refs: arrange_kernel(table.shape[0] // 2, *refs),
        out_shape=jax.ShapeDtypeStruct((rows * len(blocks), cols), BF16),
        in_specs=[spec_smem()] * 2 + [pl.BlockSpec(memory_space=pltpu.VMEM)] * len(blocks),
        out_specs=pl.BlockSpec(memory_space=pltpu.VMEM),
        compiler_params=params(),
        cost_estimate=cost(0, 4 * rows * cols * len(blocks)),
        name="arrange_rows",
    )(group, table, *blocks)


def backward_kernel(row_block, scales_ref, grad_ref, codes_ref, out_ref, weight_ref):
    row0 = row_block + pl.program_id(0) * (codes_ref.shape[0] // BLOCK)
    dequantize_into(weight_ref, codes_ref, scales_ref, row0, 0)
    out_ref[...] = lax.dot_general(
        grad_ref[...], weight_ref[...], (((1,), (1,)), ((), ())), preferred_element_type=F32
    ).astype(BF16)


def backward_product(grad_rows, codes, scales, start, cols, tile):
    tokens, depth = grad_rows.shape
    return pl.pallas_call(
        lambda *refs: backward_kernel(start // BLOCK, *refs),
        grid=(cols // tile,),
        out_shape=pltpu.HBM((tokens, cols), BF16),
        in_specs=[
            spec_smem(),
            pl.BlockSpec((tokens, depth), lambda i: (0, 0)),
            pl.BlockSpec((tile, depth), lambda i: (start // tile + i, 0)),
        ],
        out_specs=pl.BlockSpec((tokens, tile), lambda i: (0, i)),
        scratch_shapes=[pltpu.VMEM((tile, depth), BF16)],
        compiler_params=params(),
        cost_estimate=cost(
            2 * tokens * depth * cols, 2 * (tokens * depth + (depth + tokens) * cols)
        ),
        name="backward_product",
    )(scales, grad_rows, codes)


def forward_kernel(count, bits, row_block, has_sum, group_ref, order_ref, scales_ref, *refs):
    blocks, codes_ref = refs[:count], refs[count]
    sum_ref = refs[count + 1] if has_sum else None
    out_ref, rows_ref, weight_ref = refs[-3:]
    tile = codes_ref.shape[1]

    @pl.when(pl.program_id(0) == 0)
    def _():
        per = max(1, count >> bits)
        for r, block in enumerate(blocks):
            size = block.shape[0]
            offset = order_ref[r] // per ^ group_ref[0]
            turned = sum((offset >> i & 1) << bits - 1 - i for i in range(bits))
            start = (turned * per + order_ref[r] % per) * size
            rows_ref[pl.ds(pl.multiple_of(start, size), size), :] = block[...]

    dequantize_into(
        weight_ref, codes_ref, scales_ref, row_block, pl.program_id(0) * (tile // BLOCK)
    )
    total = jnp.dot(rows_ref[...], weight_ref[...], preferred_element_type=F32)
    if has_sum:
        total = total + sum_ref[...]
    out_ref[...] = total.astype(out_ref.dtype)


def forward_product(blocks, bits, group, order, codes, scales, start, running, out_dtype):
    size, depth = blocks[0].shape
    tokens, width = size * len(blocks), codes.shape[1]
    tile = min(256, width)
    sums = [] if running is None else [running]
    sliced = pl.BlockSpec((tokens, tile), lambda i: (0, i))
    return pl.pallas_call(
        lambda *refs: forward_kernel(len(blocks), bits, start // BLOCK, bool(sums), *refs),
        grid=(width // tile,),
        out_shape=pltpu.HBM((tokens, width), out_dtype),
        in_specs=[
            spec_smem(),
            spec_smem(),
            spec_smem(),
            *[
                pl.BlockSpec((size, depth), lambda i: (0, 0), pipeline_mode=pl.Buffered(1))
            ] * len(blocks),
            pl.BlockSpec((pl.Element(depth), pl.Element(tile)), lambda i: (start, i * tile)),
            *[sliced] * len(sums),
        ],
        out_specs=sliced,
        scratch_shapes=[pltpu.VMEM((tokens, depth), BF16), pltpu.VMEM((depth, tile), BF16)],
        compiler_params=params(),
        cost_estimate=cost(
            2 * tokens * depth * width, 2 * (tokens + width) * depth + 8 * tokens * width
        ),
        name="forward_product",
    )(group, order, scales, *blocks, codes, *sums)


def shares(units, parts):
    ends = [round(units * sum(parts[: i + 1]) / sum(parts)) for i in range(len(parts))]
    return [end - begin for begin, end in zip([0, *ends], ends)]


def stream_columns(sizes, tile):
    starts = np.cumsum([0, *sizes[:-1]])
    return [(int(a) * tile, int(b) * tile) for a, b in zip(starts, sizes)]


class Ring:
    def __init__(self, count, send, long_way):
        self.count, self.send = count, send
        self.reach = {long_way: count // 2, -long_way: count - 1 - count // 2}
        self.hops = {1: 0, -1: 0}

    def advance(self, step, *tokens):
        moving = self.outgoing(step)
        self.hops[step] += 1
        arrived = self.send(after(moving, *tokens), step)
        self.incoming(step, arrived)
        return arrived


class Gather(Ring):
    def __init__(self, count, send, long_way, own):
        super().__init__(count, send, long_way)
        self.blocks = {0: own}

    def outgoing(self, step):
        return self.blocks[self.hops[step] * step % self.count]

    def incoming(self, step, arrived):
        self.blocks[self.hops[step] * step % self.count] = arrived

    def all_blocks(self):
        return [self.blocks[r] for r in range(self.count)]


class Scatter(Ring):
    def __init__(self, count, send, long_way, terms):
        super().__init__(count, send, long_way)
        self.terms, self.sums = terms, {}

    def term(self, offset):
        rows = self.terms.shape[0] // self.count
        at = offset % self.count * rows
        return lax.slice_in_dim(self.terms, at, at + rows, axis=0)

    def outgoing(self, step):
        term = self.term(step * (self.reach[step] - self.hops[step]))
        if step not in self.sums:
            return term
        return (self.sums[step].astype(F32) + term.astype(F32)).astype(BF16)

    def incoming(self, step, arrived):
        self.sums[step] = arrived

    def total(self, *tokens):
        parts = [after(part, *tokens) for part in (self.term(0), *self.sums.values())]
        return sum(part.astype(F32) for part in parts).astype(BF16)


def on_device(gate_act, up_act, down_codes, down_scales, grad_out):
    groups, ring = lax.axis_size("tensor"), lax.axis_size("dp")
    group, member = lax.axis_index("tensor"), lax.axis_index("dp")
    bits = list(reversed(range(groups.bit_length() - 1)))
    rows, hidden_units = gate_act.shape
    tile = 256 if hidden_units % 256 == 0 else BLOCK
    units = hidden_units // tile
    ahead_streams = stream_columns(shares(units, AHEAD), tile)
    back_streams = stream_columns(shares(units, BACK), tile)
    cycle = ring_cycle(ring)
    table = lax.dynamic_index_in_dim(jnp.asarray(ring_tables(ring)), member, 0, keepdims=False)

    def send(value, step):
        return lax.ppermute(
            value, "dp", [(cycle[i], cycle[(i + step) % ring]) for i in range(ring)]
        )

    def partner(value, bit):
        return lax.ppermute(value, "tensor", [(i, i ^ 1 << bit) for i in range(groups)])

    def sign(bit):
        return jnp.where(group >> bit & 1 == 1, -1.0, 1.0).astype(F32)

    def paired(own, other, bit):
        return (own.astype(F32) * sign(bit) + other.astype(F32)).astype(BF16)

    group_index = group.astype(jnp.int32).reshape(1)
    last_sign = sign(bits[-1]).reshape(1)
    mix = jnp.asarray(sylvester(BLOCK), BF16)
    scale = 1.0 / math.sqrt(groups * BLOCK)

    def hidden(start, size):
        gate = lax.slice_in_dim(gate_act, start, start + size, axis=1).astype(F32)
        up = lax.slice_in_dim(up_act, start, start + size, axis=1).astype(F32)
        return (gate * jax.nn.sigmoid(gate) * up).astype(BF16)

    def exchanged(own, token, later=()):
        own = after(own, *token)
        other = arrived = partner(own, bits[0])
        other = after(other, *later)
        for previous, bit in zip(bits, bits[1:]):
            own = paired(own, other, previous)
            other = partner(own, bit)
        return own, other, arrived

    last = ring // 2
    gathers, token, seen, later = [], [], [], []
    for k, (start, size) in enumerate(ahead_streams):
        if k == 1:
            later = hop
        if k == 2:
            for _ in range(3, last):
                later = [gathers[0].advance(step, rotated) for step in (1, -1)]
            later += [gathers[0].advance(1)]
        own, other, arrived = exchanged(hidden(start, size), token, later)
        if k == 1:
            seen = [gathers[0].advance(step) for step in (1, -1)]
        if k == 2:
            seen = hop
        rotated = local_mix(own, after(other, *seen), last_sign, mix, scale)
        gathers.append(Gather(ring, send, -1 if k == 1 else 1, rotated))
        token = [arrived]
        if k < 2:
            hop = [gathers[k].advance(step) for step in (1, -1)]
        if k == 1:
            token += seen
    held = {0: after(grad_out, *token)}
    for bit in bits:
        held.update({o ^ 1 << bit: partner(x, bit) for o, x in list(held.items())})
        if bit == bits[0]:
            held = {o: after(x, rotated) for o, x in held.items()}
    grad_rows = arrange_rows(held, group_index, table)
    _, ring_a, ring_b = gathers

    running, partials = [None], []

    def forward(k, *tokens):
        running.append(
            forward_product(
                gathers[k].all_blocks(),
                len(bits),
                group_index,
                after(table, *tokens),
                down_codes,
                down_scales,
                ahead_streams[k][0],
                running[-1],
                BF16 if k == len(gathers) - 1 else F32,
            )
        )
        return running[-1]

    def backward(k, *tokens):
        start, cols = back_streams[k]
        partials.append(
            backward_product(after(grad_rows, *tokens), down_codes, down_scales, start, cols, tile)
        )
        return partials[-1]

    done = {"hops": [*hop, rotated], "work": []}

    def level(hops, work=None, *tokens):
        before = [*done["hops"], *done["work"]]
        done["hops"] = [current.advance(step, *done["work"], *tokens) for current, step in hops]
        done["work"] = [work[0](*work[1:], *before)] if work else []

    both = [(ring_a, -1), (ring_b, 1), (ring_a, 1), (ring_b, -1)]
    work = [(forward, 0), (backward, 0)]
    for _ in range(2, last):
        level(both, work.pop(0) if work else None)
    sum_a = Scatter(ring, send, 1, partials[0])
    level([(ring_b, 1), (ring_a, -1), (sum_a, 1), (ring_b, -1)], (backward, 1))
    sum_b = Scatter(ring, send, -1, partials[1])
    level([(ring_b, 1), (sum_a, -1), (sum_a, 1), (sum_b, -1)], (forward, 1))
    both = [(sum_a, 1), (sum_a, -1), (sum_b, 1), (sum_b, -1)]
    level(both, (forward, 2))
    layer_output = running[-1]
    def halved(value, bit, *tokens):
        kept = value.shape[0] // 2
        other = partner(after(lax.slice_in_dim(value, kept, 2 * kept, axis=0), *tokens), bit)
        own = lax.slice_in_dim(value, 0, kept, axis=0)
        return (own.astype(F32) + other.astype(F32)).astype(BF16)

    before = [*done["hops"], *done["work"]]
    for bit in reversed(bits[1:]):
        layer_output = halved(layer_output, bit, *before)
    done["hops"].append(layer_output)
    level(both, (backward, 2))
    for _ in range(4, last):
        level(both)
    small_sum = Scatter(ring, send, 1, partials[2])

    small_both = [(small_sum, 1), (small_sum, -1)]
    level([(small_sum, 1), (sum_b, 1), (sum_b, -1)])
    first = exchanged(sum_a.total(partials[2]), [])
    layer_output = halved(layer_output, bits[0], first[2])
    for _ in range(2, last):
        level(small_both)
    total = sum_b.total()
    second = exchanged(total, [layer_output])
    level(small_both, None, total)
    grads = []
    for k, (start, size) in enumerate(back_streams):
        own, other, _ = (
            (first, second)[k] if k < 2 else exchanged(small_sum.total(), [second[2]], grads)
        )
        grads = local_grads(
            own, other, last_sign, mix, scale, gate_act, up_act, start, grads
        )
    gate_grad, up_grad = grads
    return (layer_output, gate_grad, up_grad)


def solution(mesh):
    return jax.shard_map(
        on_device,
        mesh=mesh,
        in_specs=(
            P("dp", "tensor"),
            P("dp", "tensor"),
            P("tensor", "dp"),
            P("tensor", "dp"),
            P("tensor", "dp"),
        ),
        out_specs=(P("tensor", "dp"), P("dp", "tensor"), P("dp", "tensor")),
        check_vma=False,
    )
```

```python
import math

import jax
import jax.numpy as jnp
import numpy as np
from jax import lax
from jax.experimental import pallas as pl
from jax.experimental.pallas import tpu as pltpu
from jax.sharding import PartitionSpec as P

BLOCK = 128
AHEAD = (4, 11, 11)
BACK = (11, 11, 4)
VMEM_LIMIT = 40 * 1024 * 1024
F32, BF16 = jnp.float32, jnp.bfloat16


def after(value, *earlier):
    return lax.optimization_barrier((value, *earlier))[0]


def sylvester(order):
    matrix = np.ones((1, 1), np.float32)
    while matrix.shape[0] < order:
        matrix = np.block([[matrix, matrix], [matrix, -matrix]])
    return matrix


def ring_cycle(count):
    return [*range(0, count, 2), *reversed(range(1, count, 2))]


def ring_tables(count):
    cycle = ring_cycle(count)
    place = np.argsort(cycle)
    behind = [[cycle[(place[i] - r) % count] for r in range(count)] for i in range(count)]
    ahead = [[(place[j] - place[i]) % count for j in range(count)] for i in range(count)]
    return np.concatenate([behind, ahead], axis=1).astype(np.int32)


def params():
    return pltpu.CompilerParams(vmem_limit_bytes=VMEM_LIMIT)


def cost(operations, moved):
    return pl.CostEstimate(
        flops=operations // 16, bytes_accessed=moved // 16, transcendentals=0
    )


def spec_smem():
    return pl.BlockSpec(memory_space=pltpu.SMEM)


def dequantize_into(weight_ref, codes_ref, scales_ref, row0, col0):
    for i in range(codes_ref.shape[0] // BLOCK):
        for j in range(codes_ref.shape[1] // BLOCK):
            at = (pl.ds(i * BLOCK, BLOCK), pl.ds(j * BLOCK, BLOCK))
            wide = codes_ref[at].astype(F32) * scales_ref[row0 + i, col0 + j]
            weight_ref[at] = wide.astype(BF16)


def mixed(values, mix, scale):
    high = values.astype(BF16)
    low = (values - high.astype(F32)).astype(BF16)
    total = jnp.dot(high, mix, preferred_element_type=F32) + jnp.dot(
        low, mix, preferred_element_type=F32
    )
    return (total * scale).astype(BF16)


def mix_kernel(scale, sign_ref, mix_ref, own_ref, other_ref, out_ref):
    for j in range(own_ref.shape[1] // BLOCK):
        at = (slice(None), pl.ds(j * BLOCK, BLOCK))
        values = own_ref[at].astype(F32) * sign_ref[0] + other_ref[at].astype(F32)
        out_ref[at] = mixed(values, mix_ref[...], scale)


def local_mix(own, other, sign, mix, scale):
    rows, cols = own.shape
    return pl.pallas_call(
        lambda *refs: mix_kernel(scale, *refs),
        out_shape=jax.ShapeDtypeStruct((rows, cols), BF16),
        in_specs=[spec_smem()] + [pl.BlockSpec(memory_space=pltpu.VMEM)] * 3,
        out_specs=pl.BlockSpec(memory_space=pltpu.VMEM),
        compiler_params=params(),
        cost_estimate=cost(4 * rows * cols * BLOCK, 6 * rows * cols),
        name="local_mix",
    )(sign, mix, own, other)


def grads_kernel(scale, tile, sign_ref, mix_ref, own_ref, other_ref, gate_ref, up_ref, *refs):
    gate_grad_ref, up_grad_ref = refs[-2:]
    for j in range(tile // BLOCK):
        at = (slice(None), pl.ds(j * BLOCK, BLOCK))
        values = own_ref[at].astype(F32) * sign_ref[0] + other_ref[at].astype(F32)
        grad = mixed(values, mix_ref[...], scale).astype(F32)
        gate = gate_ref[at].astype(F32)
        sigmoid = jax.nn.sigmoid(gate)
        up_grad_ref[at] = (grad * (gate * sigmoid)).astype(BF16)
        gate_grad_ref[at] = (
            grad * up_ref[at].astype(F32) * sigmoid * (1.0 + gate * (1.0 - sigmoid))
        ).astype(BF16)


def local_grads(own, other, sign, mix, scale, gate_act, up_act, start, made):
    rows, cols = own.shape
    tile = math.gcd(start, cols)
    if tile % (2 * BLOCK) == 0:
        tile //= 2
    whole = pl.BlockSpec((rows, tile), lambda i: (0, start // tile + i))
    part = pl.BlockSpec((rows, tile), lambda i: (0, i))
    rest = [pl.BlockSpec(memory_space=pl.ANY)] * len(made)
    return pl.pallas_call(
        lambda *refs: grads_kernel(scale, tile, *refs),
        grid=(cols // tile,),
        out_shape=[jax.ShapeDtypeStruct(gate_act.shape, BF16)] * 2,
        in_specs=[
            spec_smem(),
            pl.BlockSpec((BLOCK, BLOCK), lambda i: (0, 0)),
            part,
            part,
            whole,
            whole,
            *rest,
        ],
        out_specs=[whole, whole],
        input_output_aliases={6 + k: k for k in range(len(made))},
        compiler_params=params(),
        cost_estimate=cost(4 * rows * cols * BLOCK, 12 * rows * cols),
        name="local_grads",
    )(sign, mix, own, other, gate_act, up_act, *made)


def arrange_kernel(count, group_ref, table_ref, *refs):
    out_ref = refs[-1]
    rows = out_ref.shape[0] // count
    for offset, block in enumerate(refs[:-1]):
        per = block.shape[0] // rows
        for i in range(per):
            place = table_ref[count + (group_ref[0] ^ offset) * per + i]
            start = pl.multiple_of(place * rows, rows)
            out_ref[pl.ds(start, rows), :] = block[pl.ds(i * rows, rows), :]


def arrange_rows(held, group, table):
    blocks = [held[offset] for offset in range(len(held))]
    rows, cols = blocks[0].shape
    return pl.pallas_call(
        lambda *refs: arrange_kernel(table.shape[0] // 2, *refs),
        out_shape=jax.ShapeDtypeStruct((rows * len(blocks), cols), BF16),
        in_specs=[spec_smem()] * 2 + [pl.BlockSpec(memory_space=pltpu.VMEM)] * len(blocks),
        out_specs=pl.BlockSpec(memory_space=pltpu.VMEM),
        compiler_params=params(),
        cost_estimate=cost(0, 4 * rows * cols * len(blocks)),
        name="arrange_rows",
    )(group, table, *blocks)


def backward_kernel(row_block, scales_ref, grad_ref, codes_ref, out_ref, weight_ref):
    row0 = row_block + pl.program_id(0) * (codes_ref.shape[0] // BLOCK)
    dequantize_into(weight_ref, codes_ref, scales_ref, row0, 0)
    out_ref[...] = lax.dot_general(
        grad_ref[...], weight_ref[...], (((1,), (1,)), ((), ())), preferred_element_type=F32
    ).astype(BF16)


def backward_product(grad_rows, codes, scales, start, cols, tile):
    tokens, depth = grad_rows.shape
    if start % (2 * tile) == 0 and cols % (2 * tile) == 0:
        tile *= 2
    return pl.pallas_call(
        lambda *refs: backward_kernel(start // BLOCK, *refs),
        grid=(cols // tile,),
        out_shape=pltpu.HBM((tokens, cols), BF16),
        in_specs=[
            spec_smem(),
            pl.BlockSpec((tokens, depth), lambda i: (0, 0)),
            pl.BlockSpec((tile, depth), lambda i: (start // tile + i, 0)),
        ],
        out_specs=pl.BlockSpec((tokens, tile), lambda i: (0, i)),
        scratch_shapes=[pltpu.VMEM((tile, depth), BF16)],
        compiler_params=params(),
        cost_estimate=cost(
            2 * tokens * depth * cols, 2 * (tokens * depth + (depth + tokens) * cols)
        ),
        name="backward_product",
    )(scales, grad_rows, codes)


def forward_kernel(counts, bits, row_block, has_sum, group_ref, order_ref, scales_ref, *refs):
    total_blocks = sum(counts)
    blocks, codes_ref = refs[:total_blocks], refs[total_blocks]
    sum_ref = refs[total_blocks + 1] if has_sum else None
    out_ref, rows_ref, weight_ref, sems = refs[-4:]
    tile = codes_ref.shape[1]
    per = max(1, counts[0] >> bits)
    step = pl.program_id(0)

    def copies():
        column = 0
        for part, count in enumerate(counts):
            for r in range(count):
                i = part * count + r
                size, width = blocks[i].shape
                offset = order_ref[r] // per ^ group_ref[0]
                turned = sum((offset >> k & 1) << bits - 1 - k for k in range(bits))
                start = pl.multiple_of((turned * per + order_ref[r] % per) * size, size)
                place = rows_ref.at[pl.ds(start, size), pl.ds(column, width)]
                yield pltpu.make_async_copy(blocks[i], place, sems.at[i])
            column += blocks[part * count].shape[1]

    @pl.when(step == 0)
    def _():
        for copy in copies():
            copy.start()

    dequantize_into(weight_ref, codes_ref, scales_ref, row_block, step * (tile // BLOCK))

    @pl.when(step == 0)
    def _():
        for copy in copies():
            copy.wait()

    total = jnp.dot(rows_ref[...], weight_ref[...], preferred_element_type=F32)
    if has_sum:
        total = total + sum_ref[...]
    out_ref[...] = total.astype(out_ref.dtype)


def forward_product(parts, bits, group, order, codes, scales, start, running, out_dtype):
    size, count = parts[0][0].shape[0], len(parts[0])
    depth = sum(blocks[0].shape[1] for blocks in parts)
    tokens, width = size * count, codes.shape[1]
    tile = min(512, width)
    sums = [] if running is None else [running]
    sliced = pl.BlockSpec((tokens, tile), lambda i: (0, i))
    return pl.pallas_call(
        lambda *refs: forward_kernel(
            [count] * len(parts), bits, start // BLOCK, bool(sums), *refs
        ),
        grid=(width // tile,),
        out_shape=pltpu.HBM((tokens, width), out_dtype),
        in_specs=[
            spec_smem(),
            spec_smem(),
            spec_smem(),
            *[pl.BlockSpec(memory_space=pltpu.HBM)] * (count * len(parts)),
            pl.BlockSpec((pl.Element(depth), pl.Element(tile)), lambda i: (start, i * tile)),
            *[sliced] * len(sums),
        ],
        out_specs=sliced,
        scratch_shapes=[
            pltpu.VMEM((tokens, depth), BF16),
            pltpu.VMEM((depth, tile), BF16),
            pltpu.SemaphoreType.DMA((count * len(parts),)),
        ],
        compiler_params=params(),
        cost_estimate=cost(
            2 * tokens * depth * width, 2 * (tokens + width) * depth + 8 * tokens * width
        ),
        name="forward_product",
    )(group, order, scales, *[block for blocks in parts for block in blocks], codes, *sums)


def shares(units, parts):
    ends = [round(units * sum(parts[: i + 1]) / sum(parts)) for i in range(len(parts))]
    return [end - begin for begin, end in zip([0, *ends], ends)]


def stream_columns(sizes, tile):
    starts = np.cumsum([0, *sizes[:-1]])
    return [(int(a) * tile, int(b) * tile) for a, b in zip(starts, sizes)]


class Ring:
    def __init__(self, count, send, long_way):
        self.count, self.send = count, send
        self.reach = {long_way: count // 2, -long_way: count - 1 - count // 2}
        self.hops = {1: 0, -1: 0}

    def advance(self, step, *tokens):
        moving = self.outgoing(step)
        self.hops[step] += 1
        arrived = self.send(after(moving, *tokens), step)
        self.incoming(step, arrived)
        return arrived


class Gather(Ring):
    def __init__(self, count, send, long_way, own):
        super().__init__(count, send, long_way)
        self.blocks = {0: own}

    def outgoing(self, step):
        return self.blocks[self.hops[step] * step % self.count]

    def incoming(self, step, arrived):
        self.blocks[self.hops[step] * step % self.count] = arrived

    def all_blocks(self):
        return [self.blocks[r] for r in range(self.count)]


class Scatter(Ring):
    def __init__(self, count, send, long_way, terms):
        super().__init__(count, send, long_way)
        self.terms, self.sums = terms, {}

    def term(self, offset):
        rows = self.terms.shape[0] // self.count
        at = offset % self.count * rows
        return lax.slice_in_dim(self.terms, at, at + rows, axis=0)

    def outgoing(self, step):
        term = self.term(step * (self.reach[step] - self.hops[step]))
        if step not in self.sums:
            return term
        return (self.sums[step].astype(F32) + term.astype(F32)).astype(BF16)

    def incoming(self, step, arrived):
        self.sums[step] = arrived

    def total(self, *tokens):
        parts = [after(part, *tokens) for part in (self.term(0), *self.sums.values())]
        return sum(part.astype(F32) for part in parts).astype(BF16)


def on_device(gate_act, up_act, down_codes, down_scales, grad_out):
    groups, ring = lax.axis_size("tensor"), lax.axis_size("dp")
    group, member = lax.axis_index("tensor"), lax.axis_index("dp")
    bits = list(reversed(range(groups.bit_length() - 1)))
    rows, hidden_units = gate_act.shape
    tile = 256 if hidden_units % 256 == 0 else BLOCK
    units = hidden_units // tile
    ahead_streams = stream_columns(shares(units, AHEAD), tile)
    back_streams = stream_columns(shares(units, BACK), tile)
    cycle = ring_cycle(ring)
    table = lax.dynamic_index_in_dim(jnp.asarray(ring_tables(ring)), member, 0, keepdims=False)

    def send(value, step):
        return lax.ppermute(
            value, "dp", [(cycle[i], cycle[(i + step) % ring]) for i in range(ring)]
        )

    def partner(value, bit):
        return lax.ppermute(value, "tensor", [(i, i ^ 1 << bit) for i in range(groups)])

    def sign(bit):
        return jnp.where(group >> bit & 1 == 1, -1.0, 1.0).astype(F32)

    def paired(own, other, bit):
        return (own.astype(F32) * sign(bit) + other.astype(F32)).astype(BF16)

    group_index = group.astype(jnp.int32).reshape(1)
    last_sign = sign(bits[-1]).reshape(1)
    mix = jnp.asarray(sylvester(BLOCK), BF16)
    scale = 1.0 / math.sqrt(groups * BLOCK)

    def hidden(start, size):
        gate = lax.slice_in_dim(gate_act, start, start + size, axis=1).astype(F32)
        up = lax.slice_in_dim(up_act, start, start + size, axis=1).astype(F32)
        return (gate * jax.nn.sigmoid(gate) * up).astype(BF16)

    def exchanged(own, token, later=()):
        own = after(own, *token)
        other = arrived = partner(own, bits[0])
        other = after(other, *later)
        for previous, bit in zip(bits, bits[1:]):
            own = paired(own, other, previous)
            other = partner(own, bit)
        return own, other, arrived

    last = ring // 2
    gathers, token, seen, later = [], [], [], []
    for k, (start, size) in enumerate(ahead_streams):
        if k == 1:
            later = hop
        if k == 2:
            for _ in range(3, last):
                later = [gathers[0].advance(step, rotated) for step in (1, -1)]
            later += [gathers[0].advance(1)]
        own, other, arrived = exchanged(hidden(start, size), token, later)
        if k == 1:
            seen = [gathers[0].advance(step) for step in (1, -1)]
        if k == 2:
            seen = hop
        rotated = local_mix(own, after(other, *seen), last_sign, mix, scale)
        gathers.append(Gather(ring, send, -1 if k == 1 else 1, rotated))
        token = [arrived]
        if k < 2:
            hop = [gathers[k].advance(step) for step in (1, -1)]
        if k == 1:
            token += seen
    own = after(grad_out, *token)
    held = {0: own, 1 << bits[0]: partner(own, bits[0])}
    _, ring_a, ring_b = gathers

    running, partials = [None], []

    def forward(which, *tokens):
        running.append(
            forward_product(
                [gathers[k].all_blocks() for k in which],
                len(bits),
                group_index,
                after(table, *tokens),
                down_codes,
                down_scales,
                ahead_streams[which[0]][0],
                running[-1],
                BF16 if which[-1] == len(gathers) - 1 else F32,
            )
        )
        return running[-1]

    def backward(k, *tokens):
        start, cols = back_streams[k]
        partials.append(
            backward_product(after(grad_rows, *tokens), down_codes, down_scales, start, cols, tile)
        )
        return partials[-1]

    done = {"hops": [*hop, rotated], "work": []}

    def level(hops, work=None, *tokens):
        before = [*done["hops"], *done["work"]]
        done["hops"] = [current.advance(step, *done["work"], *tokens) for current, step in hops]
        done["work"] = [work[0](*work[1:], *before)] if work else []

    both = [(ring_a, -1), (ring_b, 1), (ring_a, 1), (ring_b, -1)]
    level(both)
    held = {o: after(x, rotated) for o, x in held.items()}
    for bit in bits[1:]:
        held.update({o ^ 1 << bit: partner(x, bit) for o, x in list(held.items())})
    grad_rows = arrange_rows(held, group_index, table)
    level(both, (backward, 0))
    for _ in range(4, last):
        level(both)
    sum_a = Scatter(ring, send, 1, partials[0])
    level([(ring_b, 1), (ring_a, -1), (sum_a, 1), (ring_b, -1)], (backward, 1))
    sum_b = Scatter(ring, send, -1, partials[1])
    level([(ring_b, 1), (sum_a, -1), (sum_a, 1), (sum_b, -1)], (forward, (0, 1)))
    both = [(sum_a, 1), (sum_a, -1), (sum_b, 1), (sum_b, -1)]
    level(both, (forward, (2,)))
    layer_output = running[-1]
    def halved(value, bit, *tokens):
        kept = value.shape[0] // 2
        other = partner(after(lax.slice_in_dim(value, kept, 2 * kept, axis=0), *tokens), bit)
        own = lax.slice_in_dim(value, 0, kept, axis=0)
        return (own.astype(F32) + other.astype(F32)).astype(BF16)

    before = [*done["hops"], *done["work"]]
    for bit in reversed(bits[1:]):
        layer_output = halved(layer_output, bit, *before)
    done["hops"].append(layer_output)
    level(both, (backward, 2))
    for _ in range(4, last):
        level(both)
    small_sum = Scatter(ring, send, 1, partials[2])

    small_both = [(small_sum, 1), (small_sum, -1)]
    level([(small_sum, 1), (sum_b, 1), (sum_b, -1)])
    first = exchanged(sum_a.total(partials[2]), [])
    layer_output = halved(layer_output, bits[0], first[2])
    for _ in range(2, last):
        level(small_both)
    total = sum_b.total()
    second = exchanged(total, [layer_output])
    level(small_both, None, total)
    grads = []
    for k, (start, size) in enumerate(back_streams):
        own, other, _ = (
            (first, second)[k] if k < 2 else exchanged(small_sum.total(), [second[2]], grads)
        )
        grads = local_grads(
            own, other, last_sign, mix, scale, gate_act, up_act, start, grads
        )
    gate_grad, up_grad = grads
    return (layer_output, gate_grad, up_grad)


def solution(mesh):
    return jax.shard_map(
        on_device,
        mesh=mesh,
        in_specs=(
            P("dp", "tensor"),
            P("dp", "tensor"),
            P("tensor", "dp"),
            P("tensor", "dp"),
            P("tensor", "dp"),
        ),
        out_specs=(P("tensor", "dp"), P("dp", "tensor"), P("dp", "tensor")),
        check_vma=False,
    )
```

```python
import math

import jax
import jax.numpy as jnp
import numpy as np
from jax import lax
from jax.experimental import pallas as pl
from jax.experimental.pallas import tpu as pltpu
from jax.sharding import PartitionSpec as P

BLOCK = 128
AHEAD = (4, 11, 11)
BACK = (11, 11, 4)
VMEM_LIMIT = 40 * 1024 * 1024
F32, BF16 = jnp.float32, jnp.bfloat16


def after(value, *earlier):
    return lax.optimization_barrier((value, *earlier))[0]


def sylvester(order):
    matrix = np.ones((1, 1), np.float32)
    while matrix.shape[0] < order:
        matrix = np.block([[matrix, matrix], [matrix, -matrix]])
    return matrix


def ring_cycle(count):
    return [*range(0, count, 2), *reversed(range(1, count, 2))]


def ring_tables(count):
    cycle = ring_cycle(count)
    place = np.argsort(cycle)
    behind = [[cycle[(place[i] - r) % count] for r in range(count)] for i in range(count)]
    ahead = [[(place[j] - place[i]) % count for j in range(count)] for i in range(count)]
    return np.concatenate([behind, ahead], axis=1).astype(np.int32)


def params():
    return pltpu.CompilerParams(vmem_limit_bytes=VMEM_LIMIT)


def cost(operations, moved):
    return pl.CostEstimate(
        flops=operations // 16, bytes_accessed=moved // 16, transcendentals=0
    )


def spec_smem():
    return pl.BlockSpec(memory_space=pltpu.SMEM)


def dequantize_into(weight_ref, codes_ref, scales_ref, row0, col0):
    for i in range(codes_ref.shape[0] // BLOCK):
        for j in range(codes_ref.shape[1] // BLOCK):
            at = (pl.ds(i * BLOCK, BLOCK), pl.ds(j * BLOCK, BLOCK))
            wide = codes_ref[at].astype(F32) * scales_ref[row0 + i, col0 + j]
            weight_ref[at] = wide.astype(BF16)


def mixed(values, mix, scale):
    high = values.astype(BF16)
    low = (values - high.astype(F32)).astype(BF16)
    total = jnp.dot(high, mix, preferred_element_type=F32) + jnp.dot(
        low, mix, preferred_element_type=F32
    )
    return (total * scale).astype(BF16)


def mix_kernel(scale, sign_ref, mix_ref, own_ref, other_ref, out_ref):
    for j in range(own_ref.shape[1] // BLOCK):
        at = (slice(None), pl.ds(j * BLOCK, BLOCK))
        values = own_ref[at].astype(F32) * sign_ref[0] + other_ref[at].astype(F32)
        out_ref[at] = mixed(values, mix_ref[...], scale)


def local_mix(own, other, sign, mix, scale):
    rows, cols = own.shape
    return pl.pallas_call(
        lambda *refs: mix_kernel(scale, *refs),
        out_shape=jax.ShapeDtypeStruct((rows, cols), BF16),
        in_specs=[spec_smem()] + [pl.BlockSpec(memory_space=pltpu.VMEM)] * 3,
        out_specs=pl.BlockSpec(memory_space=pltpu.VMEM),
        compiler_params=params(),
        cost_estimate=cost(4 * rows * cols * BLOCK, 6 * rows * cols),
        name="local_mix",
    )(sign, mix, own, other)


def grads_kernel(scale, tile, sign_ref, mix_ref, own_ref, other_ref, gate_ref, up_ref, *refs):
    gate_grad_ref, up_grad_ref = refs[-2:]
    for j in range(tile // BLOCK):
        at = (slice(None), pl.ds(j * BLOCK, BLOCK))
        values = own_ref[at].astype(F32) * sign_ref[0] + other_ref[at].astype(F32)
        grad = mixed(values, mix_ref[...], scale).astype(F32)
        gate = gate_ref[at].astype(F32)
        sigmoid = jax.nn.sigmoid(gate)
        up_grad_ref[at] = (grad * (gate * sigmoid)).astype(BF16)
        gate_grad_ref[at] = (
            grad * up_ref[at].astype(F32) * sigmoid * (1.0 + gate * (1.0 - sigmoid))
        ).astype(BF16)


def local_grads(own, other, sign, mix, scale, gate_act, up_act, start, made):
    rows, cols = own.shape
    tile = math.gcd(start, cols)
    if tile % (2 * BLOCK) == 0:
        tile //= 2
    whole = pl.BlockSpec((rows, tile), lambda i: (0, start // tile + i))
    part = pl.BlockSpec((rows, tile), lambda i: (0, i))
    rest = [pl.BlockSpec(memory_space=pl.ANY)] * len(made)
    return pl.pallas_call(
        lambda *refs: grads_kernel(scale, tile, *refs),
        grid=(cols // tile,),
        out_shape=[jax.ShapeDtypeStruct(gate_act.shape, BF16)] * 2,
        in_specs=[
            spec_smem(),
            pl.BlockSpec((BLOCK, BLOCK), lambda i: (0, 0)),
            part,
            part,
            whole,
            whole,
            *rest,
        ],
        out_specs=[whole, whole],
        input_output_aliases={6 + k: k for k in range(len(made))},
        compiler_params=params(),
        cost_estimate=cost(4 * rows * cols * BLOCK, 12 * rows * cols),
        name="local_grads",
    )(sign, mix, own, other, gate_act, up_act, *made)


def arrange_kernel(count, group_ref, table_ref, *refs):
    out_ref = refs[-1]
    rows = out_ref.shape[0] // count
    for offset, block in enumerate(refs[:-1]):
        per = block.shape[0] // rows
        for i in range(per):
            place = table_ref[count + (group_ref[0] ^ offset) * per + i]
            start = pl.multiple_of(place * rows, rows)
            out_ref[pl.ds(start, rows), :] = block[pl.ds(i * rows, rows), :]


def arrange_rows(held, group, table):
    blocks = [held[offset] for offset in range(len(held))]
    rows, cols = blocks[0].shape
    return pl.pallas_call(
        lambda *refs: arrange_kernel(table.shape[0] // 2, *refs),
        out_shape=jax.ShapeDtypeStruct((rows * len(blocks), cols), BF16),
        in_specs=[spec_smem()] * 2 + [pl.BlockSpec(memory_space=pltpu.VMEM)] * len(blocks),
        out_specs=pl.BlockSpec(memory_space=pltpu.VMEM),
        compiler_params=params(),
        cost_estimate=cost(0, 4 * rows * cols * len(blocks)),
        name="arrange_rows",
    )(group, table, *blocks)


def backward_kernel(row_block, scales_ref, grad_ref, codes_ref, out_ref, weight_ref):
    row0 = row_block + pl.program_id(0) * (codes_ref.shape[0] // BLOCK)
    dequantize_into(weight_ref, codes_ref, scales_ref, row0, 0)
    out_ref[...] = lax.dot_general(
        grad_ref[...], weight_ref[...], (((1,), (1,)), ((), ())), preferred_element_type=F32
    ).astype(BF16)


def backward_product(grad_rows, codes, scales, start, cols, tile):
    tokens, depth = grad_rows.shape
    if start % (2 * tile) == 0 and cols % (2 * tile) == 0:
        tile *= 2
    return pl.pallas_call(
        lambda *refs: backward_kernel(start // BLOCK, *refs),
        grid=(cols // tile,),
        out_shape=pltpu.HBM((tokens, cols), BF16),
        in_specs=[
            spec_smem(),
            pl.BlockSpec((tokens, depth), lambda i: (0, 0)),
            pl.BlockSpec((tile, depth), lambda i: (start // tile + i, 0)),
        ],
        out_specs=pl.BlockSpec((tokens, tile), lambda i: (0, i)),
        scratch_shapes=[pltpu.VMEM((tile, depth), BF16)],
        compiler_params=params(),
        cost_estimate=cost(
            2 * tokens * depth * cols, 2 * (tokens * depth + (depth + tokens) * cols)
        ),
        name="backward_product",
    )(scales, grad_rows, codes)


def forward_kernel(counts, bits, row_block, has_sum, group_ref, order_ref, scales_ref, *refs):
    total_blocks = sum(counts)
    blocks, codes_ref = refs[:total_blocks], refs[total_blocks]
    rows_ref, weight_ref, sems, sum_tile_ref, sum_sem = refs[-5:]
    out_refs = refs[total_blocks + 1 + has_sum : -5]
    tile = codes_ref.shape[1]
    per = max(1, counts[0] >> bits)
    step = pl.program_id(0)

    def copies():
        column = 0
        for part, count in enumerate(counts):
            for r in range(count):
                i = part * count + r
                size, width = blocks[i].shape
                offset = order_ref[r] // per ^ group_ref[0]
                turned = sum((offset >> k & 1) << bits - 1 - k for k in range(bits))
                start = pl.multiple_of((turned * per + order_ref[r] % per) * size, size)
                place = rows_ref.at[pl.ds(start, size), pl.ds(column, width)]
                yield pltpu.make_async_copy(blocks[i], place, sems.at[i])
            column += blocks[part * count].shape[1]

    def sum_copy():
        columns = pl.ds(pl.multiple_of(step * tile, tile), tile)
        sum_ref = refs[total_blocks + 1]
        return pltpu.make_async_copy(sum_ref.at[:, columns], sum_tile_ref, sum_sem)

    @pl.when(step == 0)
    def _():
        for copy in copies():
            copy.start()

    if has_sum:
        sum_copy().start()
    dequantize_into(weight_ref, codes_ref, scales_ref, row_block, step * (tile // BLOCK))

    @pl.when(step == 0)
    def _():
        for copy in copies():
            copy.wait()

    total = jnp.dot(rows_ref[...], weight_ref[...], preferred_element_type=F32)
    if has_sum:
        sum_copy().wait()
        total = total + sum_tile_ref[...]
    size = total.shape[0] // len(out_refs)
    for i, out_ref in enumerate(out_refs):
        out_ref[...] = total[i * size : (i + 1) * size].astype(out_ref.dtype)


def forward_product(parts, bits, group, order, codes, scales, start, running, final):
    size, count = parts[0][0].shape[0], len(parts[0])
    depth = sum(blocks[0].shape[1] for blocks in parts)
    tokens, width = size * count, codes.shape[1]
    tile = min(256, width)
    sums = [] if running is None else [running]
    halves = 2 if final else 1
    made = jax.ShapeDtypeStruct((tokens // halves, width), BF16 if final else F32)
    return pl.pallas_call(
        lambda *refs: forward_kernel(
            [count] * len(parts), bits, start // BLOCK, len(sums), *refs
        ),
        grid=(width // tile,),
        out_shape=[pltpu.HBM(made.shape, made.dtype)] * halves,
        in_specs=[
            spec_smem(),
            spec_smem(),
            spec_smem(),
            *[pl.BlockSpec(memory_space=pltpu.HBM)] * (count * len(parts)),
            pl.BlockSpec((pl.Element(depth), pl.Element(tile)), lambda i: (start, i * tile)),
            *[pl.BlockSpec(memory_space=pltpu.HBM)] * len(sums),
        ],
        out_specs=[pl.BlockSpec((made.shape[0], tile), lambda i: (0, i))] * halves,
        scratch_shapes=[
            pltpu.VMEM((tokens, depth), BF16),
            pltpu.VMEM((depth, tile), BF16),
            pltpu.SemaphoreType.DMA((count * len(parts),)),
            pltpu.VMEM((tokens, tile), F32),
            pltpu.SemaphoreType.DMA,
        ],
        compiler_params=params(),
        cost_estimate=cost(
            2 * tokens * depth * width, 2 * (tokens + width) * depth + 8 * tokens * width
        ),
        name="forward_product",
    )(group, order, scales, *[block for blocks in parts for block in blocks], codes, *sums)


def shares(units, parts):
    ends = [round(units * sum(parts[: i + 1]) / sum(parts)) for i in range(len(parts))]
    return [end - begin for begin, end in zip([0, *ends], ends)]


def stream_columns(sizes, tile):
    starts = np.cumsum([0, *sizes[:-1]])
    return [(int(a) * tile, int(b) * tile) for a, b in zip(starts, sizes)]


class Ring:
    def __init__(self, count, send, long_way):
        self.count, self.send = count, send
        self.reach = {long_way: count // 2, -long_way: count - 1 - count // 2}
        self.hops = {1: 0, -1: 0}

    def advance(self, step, *tokens):
        moving = self.outgoing(step)
        self.hops[step] += 1
        arrived = self.send(after(moving, *tokens), step)
        self.incoming(step, arrived)
        return arrived


class Gather(Ring):
    def __init__(self, count, send, long_way, own):
        super().__init__(count, send, long_way)
        self.blocks = {0: own}

    def outgoing(self, step):
        return self.blocks[self.hops[step] * step % self.count]

    def incoming(self, step, arrived):
        self.blocks[self.hops[step] * step % self.count] = arrived

    def all_blocks(self):
        return [self.blocks[r] for r in range(self.count)]


class Scatter(Ring):
    def __init__(self, count, send, long_way, terms):
        super().__init__(count, send, long_way)
        self.terms, self.sums = terms, {}

    def term(self, offset):
        rows = self.terms.shape[0] // self.count
        at = offset % self.count * rows
        return lax.slice_in_dim(self.terms, at, at + rows, axis=0)

    def outgoing(self, step):
        term = self.term(step * (self.reach[step] - self.hops[step]))
        if step not in self.sums:
            return term
        return (self.sums[step].astype(F32) + term.astype(F32)).astype(BF16)

    def incoming(self, step, arrived):
        self.sums[step] = arrived

    def total(self, *tokens):
        parts = [after(part, *tokens) for part in (self.term(0), *self.sums.values())]
        return sum(part.astype(F32) for part in parts).astype(BF16)


def on_device(gate_act, up_act, down_codes, down_scales, grad_out):
    groups, ring = lax.axis_size("tensor"), lax.axis_size("dp")
    group, member = lax.axis_index("tensor"), lax.axis_index("dp")
    bits = list(reversed(range(groups.bit_length() - 1)))
    rows, hidden_units = gate_act.shape
    tile = 256 if hidden_units % 256 == 0 else BLOCK
    units = hidden_units // tile
    ahead_streams = stream_columns(shares(units, AHEAD), tile)
    back_streams = stream_columns(shares(units, BACK), tile)
    cycle = ring_cycle(ring)
    table = lax.dynamic_index_in_dim(jnp.asarray(ring_tables(ring)), member, 0, keepdims=False)

    def send(value, step):
        return lax.ppermute(
            value, "dp", [(cycle[i], cycle[(i + step) % ring]) for i in range(ring)]
        )

    def partner(value, bit):
        return lax.ppermute(value, "tensor", [(i, i ^ 1 << bit) for i in range(groups)])

    def sign(bit):
        return jnp.where(group >> bit & 1 == 1, -1.0, 1.0).astype(F32)

    def paired(own, other, bit):
        return (own.astype(F32) * sign(bit) + other.astype(F32)).astype(BF16)

    group_index = group.astype(jnp.int32).reshape(1)
    last_sign = sign(bits[-1]).reshape(1)
    mix = jnp.asarray(sylvester(BLOCK), BF16)
    scale = 1.0 / math.sqrt(groups * BLOCK)

    def hidden(start, size):
        gate = lax.slice_in_dim(gate_act, start, start + size, axis=1).astype(F32)
        up = lax.slice_in_dim(up_act, start, start + size, axis=1).astype(F32)
        return (gate * jax.nn.sigmoid(gate) * up).astype(BF16)

    def exchanged(own, token, later=()):
        own = after(own, *token)
        other = arrived = partner(own, bits[0])
        other = after(other, *later)
        for previous, bit in zip(bits, bits[1:]):
            own = paired(own, other, previous)
            other = partner(own, bit)
        return own, other, arrived

    last = ring // 2
    gathers, token, seen, later = [], [], [], []
    for k, (start, size) in enumerate(ahead_streams):
        if k == 1:
            later = hop
        if k == 2:
            for _ in range(3, last):
                later = [gathers[0].advance(step, rotated) for step in (1, -1)]
            later += [gathers[0].advance(1)]
        own, other, arrived = exchanged(hidden(start, size), token, later)
        if k == 1:
            seen = [gathers[0].advance(step) for step in (1, -1)]
        if k == 2:
            seen = hop
        rotated = local_mix(own, after(other, *seen), last_sign, mix, scale)
        gathers.append(Gather(ring, send, -1 if k == 1 else 1, rotated))
        token = [arrived]
        if k < 2:
            hop = [gathers[k].advance(step) for step in (1, -1)]
        if k == 1:
            token += seen
    own = after(grad_out, *token)
    held = {0: own, 1 << bits[0]: partner(own, bits[0])}
    _, ring_a, ring_b = gathers

    running, partials = [[None]], []

    def forward(which, *tokens):
        running.append(
            forward_product(
                [gathers[k].all_blocks() for k in which],
                len(bits),
                group_index,
                after(table, *tokens),
                down_codes,
                down_scales,
                ahead_streams[which[0]][0],
                running[-1][0],
                which[-1] == len(gathers) - 1,
            )
        )
        return running[-1][0]

    def backward(k, *tokens):
        start, cols = back_streams[k]
        partials.append(
            backward_product(after(grad_rows, *tokens), down_codes, down_scales, start, cols, tile)
        )
        return partials[-1]

    done = {"hops": [*hop, rotated], "work": []}

    def level(hops, work=None, *tokens):
        before = [*done["hops"], *done["work"]]
        done["hops"] = [current.advance(step, *done["work"], *tokens) for current, step in hops]
        done["work"] = [work[0](*work[1:], *before)] if work else []

    both = [(ring_a, -1), (ring_b, 1), (ring_a, 1), (ring_b, -1)]
    level(both)
    held = {o: after(x, rotated) for o, x in held.items()}
    for bit in bits[1:]:
        held.update({o ^ 1 << bit: partner(x, bit) for o, x in list(held.items())})
    grad_rows = arrange_rows(held, group_index, table)
    level(both, (backward, 0))
    for _ in range(4, last):
        level(both)
    sum_a = Scatter(ring, send, 1, partials[0])
    level([(ring_b, 1), (ring_a, -1), (sum_a, 1), (ring_b, -1)], (backward, 1))
    sum_b = Scatter(ring, send, -1, partials[1])
    level([(ring_b, 1), (sum_a, -1), (sum_a, 1), (sum_b, -1)], (forward, (0, 1)))
    both = [(sum_a, 1), (sum_a, -1), (sum_b, 1), (sum_b, -1)]
    level(both, (forward, (2,)))
    halves = running[-1]
    def halves_of(value):
        kept = value.shape[0] // 2
        return [lax.slice_in_dim(value, at, at + kept, axis=0) for at in (0, kept)]

    def halved(halves, bit, *tokens):
        own, sent = halves
        other = partner(after(sent, *tokens), bit)
        return (own.astype(F32) + other.astype(F32)).astype(BF16)

    before = [*done["hops"], *done["work"]]
    for bit in reversed(bits[1:]):
        summed = halved(halves, bit, *before)
        halves = halves_of(summed)
    done["hops"].append(summed)
    level(both, (backward, 2))
    for _ in range(4, last):
        level(both)
    small_sum = Scatter(ring, send, 1, partials[2])

    small_both = [(small_sum, 1), (small_sum, -1)]
    level([(small_sum, 1), (sum_b, 1), (sum_b, -1)])
    first = exchanged(sum_a.total(partials[2]), [])
    layer_output = halved(halves, bits[0], first[2])
    for _ in range(2, last):
        level(small_both)
    total = sum_b.total()
    second = exchanged(total, [layer_output])
    level(small_both, None, total)
    grads = []
    for k, (start, size) in enumerate(back_streams):
        own, other, _ = (
            (first, second)[k] if k < 2 else exchanged(small_sum.total(), [second[2]], grads)
        )
        grads = local_grads(
            own, other, last_sign, mix, scale, gate_act, up_act, start, grads
        )
    gate_grad, up_grad = grads
    return (layer_output, gate_grad, up_grad)


def solution(mesh):
    return jax.shard_map(
        on_device,
        mesh=mesh,
        in_specs=(
            P("dp", "tensor"),
            P("dp", "tensor"),
            P("tensor", "dp"),
            P("tensor", "dp"),
            P("tensor", "dp"),
        ),
        out_specs=(P("tensor", "dp"), P("dp", "tensor"), P("dp", "tensor")),
        check_vma=False,
    )
```

```python
import math

import jax
import jax.numpy as jnp
import numpy as np
from jax import lax
from jax.experimental import pallas as pl
from jax.experimental.pallas import tpu as pltpu
from jax.sharding import PartitionSpec as P

BLOCK = 128
AHEAD = (5, 10, 11)
BACK = (11, 11, 4)
VMEM_LIMIT = 40 * 1024 * 1024
F32, BF16 = jnp.float32, jnp.bfloat16


def after(value, *earlier):
    return lax.optimization_barrier((value, *earlier))[0]


def sylvester(order):
    matrix = np.ones((1, 1), np.float32)
    while matrix.shape[0] < order:
        matrix = np.block([[matrix, matrix], [matrix, -matrix]])
    return matrix


def ring_cycle(count):
    return [*range(0, count, 2), *reversed(range(1, count, 2))]


def ring_tables(count):
    cycle = ring_cycle(count)
    place = np.argsort(cycle)
    behind = [[cycle[(place[i] - r) % count] for r in range(count)] for i in range(count)]
    ahead = [[(place[j] - place[i]) % count for j in range(count)] for i in range(count)]
    return np.concatenate([behind, ahead], axis=1).astype(np.int32)


def params():
    return pltpu.CompilerParams(vmem_limit_bytes=VMEM_LIMIT)


def cost(operations, moved):
    return pl.CostEstimate(
        flops=operations // 16, bytes_accessed=moved // 16, transcendentals=0
    )


def spec_smem():
    return pl.BlockSpec(memory_space=pltpu.SMEM)


def dequantize_into(weight_ref, codes_ref, scales_ref, row0, col0):
    for i in range(codes_ref.shape[0] // BLOCK):
        for j in range(codes_ref.shape[1] // BLOCK):
            at = (pl.ds(i * BLOCK, BLOCK), pl.ds(j * BLOCK, BLOCK))
            wide = codes_ref[at].astype(F32) * scales_ref[row0 + i, col0 + j]
            weight_ref[at] = wide.astype(BF16)


def mixed(values, mix, scale):
    high = values.astype(BF16)
    low = (values - high.astype(F32)).astype(BF16)
    total = jnp.dot(high, mix, preferred_element_type=F32) + jnp.dot(
        low, mix, preferred_element_type=F32
    )
    return (total * scale).astype(BF16)


def mix_kernel(scale, sign_ref, mix_ref, own_ref, other_ref, out_ref):
    for j in range(own_ref.shape[1] // BLOCK):
        at = (slice(None), pl.ds(j * BLOCK, BLOCK))
        values = own_ref[at].astype(F32) * sign_ref[0] + other_ref[at].astype(F32)
        out_ref[at] = mixed(values, mix_ref[...], scale)


def local_mix(own, other, sign, mix, scale):
    rows, cols = own.shape
    return pl.pallas_call(
        lambda *refs: mix_kernel(scale, *refs),
        out_shape=jax.ShapeDtypeStruct((rows, cols), BF16),
        in_specs=[spec_smem()] + [pl.BlockSpec(memory_space=pltpu.VMEM)] * 3,
        out_specs=pl.BlockSpec(memory_space=pltpu.VMEM),
        compiler_params=params(),
        cost_estimate=cost(4 * rows * cols * BLOCK, 6 * rows * cols),
        name="local_mix",
    )(sign, mix, own, other)


def grads_kernel(scale, tile, sign_ref, mix_ref, own_ref, other_ref, gate_ref, up_ref, *refs):
    gate_grad_ref, up_grad_ref = refs[-2:]
    for j in range(tile // BLOCK):
        at = (slice(None), pl.ds(j * BLOCK, BLOCK))
        values = own_ref[at].astype(F32) * sign_ref[0] + other_ref[at].astype(F32)
        grad = mixed(values, mix_ref[...], scale).astype(F32)
        gate = gate_ref[at].astype(F32)
        sigmoid = jax.nn.sigmoid(gate)
        up_grad_ref[at] = (grad * (gate * sigmoid)).astype(BF16)
        gate_grad_ref[at] = (
            grad * up_ref[at].astype(F32) * sigmoid * (1.0 + gate * (1.0 - sigmoid))
        ).astype(BF16)


def local_grads(own, other, sign, mix, scale, gate_act, up_act, start, made):
    rows, cols = own.shape
    tile = math.gcd(start, cols)
    if tile % (2 * BLOCK) == 0:
        tile //= 2
    whole = pl.BlockSpec((rows, tile), lambda i: (0, start // tile + i))
    part = pl.BlockSpec((rows, tile), lambda i: (0, i))
    rest = [pl.BlockSpec(memory_space=pl.ANY)] * len(made)
    return pl.pallas_call(
        lambda *refs: grads_kernel(scale, tile, *refs),
        grid=(cols // tile,),
        out_shape=[jax.ShapeDtypeStruct(gate_act.shape, BF16)] * 2,
        in_specs=[
            spec_smem(),
            pl.BlockSpec((BLOCK, BLOCK), lambda i: (0, 0)),
            part,
            part,
            whole,
            whole,
            *rest,
        ],
        out_specs=[whole, whole],
        input_output_aliases={6 + k: k for k in range(len(made))},
        compiler_params=params(),
        cost_estimate=cost(4 * rows * cols * BLOCK, 12 * rows * cols),
        name="local_grads",
    )(sign, mix, own, other, gate_act, up_act, *made)


def arrange_kernel(count, group_ref, table_ref, *refs):
    out_ref = refs[-1]
    rows = out_ref.shape[0] // count
    for offset, block in enumerate(refs[:-1]):
        per = block.shape[0] // rows
        for i in range(per):
            place = table_ref[count + (group_ref[0] ^ offset) * per + i]
            start = pl.multiple_of(place * rows, rows)
            out_ref[pl.ds(start, rows), :] = block[pl.ds(i * rows, rows), :]


def arrange_rows(held, group, table):
    blocks = [held[offset] for offset in range(len(held))]
    rows, cols = blocks[0].shape
    return pl.pallas_call(
        lambda *refs: arrange_kernel(table.shape[0] // 2, *refs),
        out_shape=jax.ShapeDtypeStruct((rows * len(blocks), cols), BF16),
        in_specs=[spec_smem()] * 2 + [pl.BlockSpec(memory_space=pltpu.VMEM)] * len(blocks),
        out_specs=pl.BlockSpec(memory_space=pltpu.VMEM),
        compiler_params=params(),
        cost_estimate=cost(0, 4 * rows * cols * len(blocks)),
        name="arrange_rows",
    )(group, table, *blocks)


def backward_kernel(row_block, scales_ref, grad_ref, codes_ref, out_ref, weight_ref):
    row0 = row_block + pl.program_id(0) * (codes_ref.shape[0] // BLOCK)
    dequantize_into(weight_ref, codes_ref, scales_ref, row0, 0)
    out_ref[...] = lax.dot_general(
        grad_ref[...], weight_ref[...], (((1,), (1,)), ((), ())), preferred_element_type=F32
    ).astype(BF16)


def backward_product(grad_rows, codes, scales, start, cols, tile):
    tokens, depth = grad_rows.shape
    if start % (2 * tile) == 0 and cols % (2 * tile) == 0:
        tile *= 2
    return pl.pallas_call(
        lambda *refs: backward_kernel(start // BLOCK, *refs),
        grid=(cols // tile,),
        out_shape=pltpu.HBM((tokens, cols), BF16),
        in_specs=[
            spec_smem(),
            pl.BlockSpec((tokens, depth), lambda i: (0, 0)),
            pl.BlockSpec((tile, depth), lambda i: (start // tile + i, 0)),
        ],
        out_specs=pl.BlockSpec((tokens, tile), lambda i: (0, i)),
        scratch_shapes=[pltpu.VMEM((tile, depth), BF16)],
        compiler_params=params(),
        cost_estimate=cost(
            2 * tokens * depth * cols, 2 * (tokens * depth + (depth + tokens) * cols)
        ),
        name="backward_product",
    )(scales, grad_rows, codes)


def forward_kernel(counts, bits, row_block, has_sum, group_ref, order_ref, scales_ref, *refs):
    total_blocks = sum(counts)
    blocks, codes_ref = refs[:total_blocks], refs[total_blocks]
    sum_ref = refs[total_blocks + 1] if has_sum else None
    out_ref, rows_ref, weight_ref, sems = refs[-4:]
    tile = codes_ref.shape[1]
    per = max(1, counts[0] >> bits)
    step = pl.program_id(0)

    def places():
        column = 0
        for part, count in enumerate(counts):
            for r in range(count):
                i = part * count + r
                size, width = blocks[i].shape
                offset = order_ref[r] // per ^ group_ref[0]
                turned = sum((offset >> k & 1) << bits - 1 - k for k in range(bits))
                start = pl.multiple_of((turned * per + order_ref[r] % per) * size, size)
                yield i, rows_ref.at[pl.ds(start, size), pl.ds(column, width)]
            column += blocks[part * count].shape[1]

    def copies():
        return [pltpu.make_async_copy(blocks[i], place, sems.at[i]) for i, place in places()]

    @pl.when(step == 0)
    def _():
        if len(counts) == 1:
            for i, place in places():
                place[...] = blocks[i][...]
        else:
            for copy in copies():
                copy.start()

    dequantize_into(weight_ref, codes_ref, scales_ref, row_block, step * (tile // BLOCK))

    if len(counts) > 1:

        @pl.when(step == 0)
        def _():
            for copy in copies():
                copy.wait()

    total = jnp.dot(rows_ref[...], weight_ref[...], preferred_element_type=F32)
    if has_sum:
        total = total + sum_ref[...]
    out_ref[...] = total.astype(out_ref.dtype)


def forward_product(parts, bits, group, order, codes, scales, start, running, out_dtype):
    size, count = parts[0][0].shape[0], len(parts[0])
    depth = sum(blocks[0].shape[1] for blocks in parts)
    tokens, width = size * count, codes.shape[1]
    tile = min(512 if len(parts) > 1 else 256, width)
    if len(parts) > 1:
        block = pl.BlockSpec(memory_space=pltpu.HBM)
    else:
        block = pl.BlockSpec((size, depth), lambda i: (0, 0), pipeline_mode=pl.Buffered(1))
    sums = [] if running is None else [running]
    sliced = pl.BlockSpec((tokens, tile), lambda i: (0, i))
    return pl.pallas_call(
        lambda *refs: forward_kernel(
            [count] * len(parts), bits, start // BLOCK, bool(sums), *refs
        ),
        grid=(width // tile,),
        out_shape=pltpu.HBM((tokens, width), out_dtype),
        in_specs=[
            spec_smem(),
            spec_smem(),
            spec_smem(),
            *[block] * (count * len(parts)),
            pl.BlockSpec((pl.Element(depth), pl.Element(tile)), lambda i: (start, i * tile)),
            *[sliced] * len(sums),
        ],
        out_specs=sliced,
        scratch_shapes=[
            pltpu.VMEM((tokens, depth), BF16),
            pltpu.VMEM((depth, tile), BF16),
            pltpu.SemaphoreType.DMA((count * len(parts),)),
        ],
        compiler_params=params(),
        cost_estimate=cost(
            2 * tokens * depth * width, 2 * (tokens + width) * depth + 8 * tokens * width
        ),
        name="forward_product",
    )(group, order, scales, *[block for blocks in parts for block in blocks], codes, *sums)


def shares(units, parts):
    ends = [round(units * sum(parts[: i + 1]) / sum(parts)) for i in range(len(parts))]
    return [end - begin for begin, end in zip([0, *ends], ends)]


def stream_columns(sizes, tile):
    starts = np.cumsum([0, *sizes[:-1]])
    return [(int(a) * tile, int(b) * tile) for a, b in zip(starts, sizes)]


class Ring:
    def __init__(self, count, send, long_way):
        self.count, self.send = count, send
        self.reach = {long_way: count // 2, -long_way: count - 1 - count // 2}
        self.hops = {1: 0, -1: 0}

    def advance(self, step, *tokens):
        moving = self.outgoing(step)
        self.hops[step] += 1
        arrived = self.send(after(moving, *tokens), step)
        self.incoming(step, arrived)
        return arrived


class Gather(Ring):
    def __init__(self, count, send, long_way, own):
        super().__init__(count, send, long_way)
        self.blocks = {0: own}

    def outgoing(self, step):
        return self.blocks[self.hops[step] * step % self.count]

    def incoming(self, step, arrived):
        self.blocks[self.hops[step] * step % self.count] = arrived

    def all_blocks(self):
        return [self.blocks[r] for r in range(self.count)]


class Scatter(Ring):
    def __init__(self, count, send, long_way, terms):
        super().__init__(count, send, long_way)
        self.terms, self.sums = terms, {}

    def term(self, offset):
        rows = self.terms.shape[0] // self.count
        at = offset % self.count * rows
        return lax.slice_in_dim(self.terms, at, at + rows, axis=0)

    def outgoing(self, step):
        term = self.term(step * (self.reach[step] - self.hops[step]))
        if step not in self.sums:
            return term
        return (self.sums[step].astype(F32) + term.astype(F32)).astype(BF16)

    def incoming(self, step, arrived):
        self.sums[step] = arrived

    def total(self, *tokens):
        parts = [after(part, *tokens) for part in (self.term(0), *self.sums.values())]
        return sum(part.astype(F32) for part in parts).astype(BF16)


def on_device(gate_act, up_act, down_codes, down_scales, grad_out):
    groups, ring = lax.axis_size("tensor"), lax.axis_size("dp")
    group, member = lax.axis_index("tensor"), lax.axis_index("dp")
    bits = list(reversed(range(groups.bit_length() - 1)))
    rows, hidden_units = gate_act.shape
    tile = 256 if hidden_units % 256 == 0 else BLOCK
    units = hidden_units // tile
    ahead_streams = stream_columns(shares(units, AHEAD), tile)
    back_streams = stream_columns(shares(units, BACK), tile)
    cycle = ring_cycle(ring)
    table = lax.dynamic_index_in_dim(jnp.asarray(ring_tables(ring)), member, 0, keepdims=False)

    def send(value, step):
        return lax.ppermute(
            value, "dp", [(cycle[i], cycle[(i + step) % ring]) for i in range(ring)]
        )

    def partner(value, bit):
        return lax.ppermute(value, "tensor", [(i, i ^ 1 << bit) for i in range(groups)])

    def sign(bit):
        return jnp.where(group >> bit & 1 == 1, -1.0, 1.0).astype(F32)

    def paired(own, other, bit):
        return (own.astype(F32) * sign(bit) + other.astype(F32)).astype(BF16)

    group_index = group.astype(jnp.int32).reshape(1)
    last_sign = sign(bits[-1]).reshape(1)
    mix = jnp.asarray(sylvester(BLOCK), BF16)
    scale = 1.0 / math.sqrt(groups * BLOCK)

    def hidden(start, size):
        gate = lax.slice_in_dim(gate_act, start, start + size, axis=1).astype(F32)
        up = lax.slice_in_dim(up_act, start, start + size, axis=1).astype(F32)
        return (gate * jax.nn.sigmoid(gate) * up).astype(BF16)

    def exchanged(own, token, later=()):
        own = after(own, *token)
        other = arrived = partner(own, bits[0])
        other = after(other, *later)
        for previous, bit in zip(bits, bits[1:]):
            own = paired(own, other, previous)
            other = partner(own, bit)
        return own, other, arrived

    last = ring // 2
    gathers, token, seen, later = [], [], [], []
    for k, (start, size) in enumerate(ahead_streams):
        if k == 1:
            later = hop
        if k == 2:
            for _ in range(3, last):
                later = [gathers[0].advance(step, rotated) for step in (1, -1)]
            later += [gathers[0].advance(1)]
        own, other, arrived = exchanged(hidden(start, size), token, later)
        if k == 1:
            seen = [gathers[0].advance(step) for step in (1, -1)]
        if k == 2:
            seen = hop
        rotated = local_mix(own, after(other, *seen), last_sign, mix, scale)
        gathers.append(Gather(ring, send, -1 if k == 1 else 1, rotated))
        token = [arrived]
        if k < 2:
            hop = [gathers[k].advance(step) for step in (1, -1)]
        if k == 1:
            token += seen
    own = after(grad_out, *token)
    held = {0: own, 1 << bits[0]: partner(own, bits[0])}
    _, ring_a, ring_b = gathers

    running, partials = [None], []

    def forward(which, *tokens):
        running.append(
            forward_product(
                [gathers[k].all_blocks() for k in which],
                len(bits),
                group_index,
                after(table, *tokens),
                down_codes,
                down_scales,
                ahead_streams[which[0]][0],
                running[-1],
                BF16 if which[-1] == len(gathers) - 1 else F32,
            )
        )
        return running[-1]

    def backward(k, *tokens):
        start, cols = back_streams[k]
        partials.append(
            backward_product(after(grad_rows, *tokens), down_codes, down_scales, start, cols, tile)
        )
        return partials[-1]

    done = {"hops": [*hop, rotated], "work": []}

    def level(hops, work=None, *tokens):
        before = [*done["hops"], *done["work"]]
        done["hops"] = [current.advance(step, *done["work"], *tokens) for current, step in hops]
        done["work"] = [work[0](*work[1:], *before)] if work else []

    both = [(ring_a, -1), (ring_b, 1), (ring_a, 1), (ring_b, -1)]
    level(both)
    held = {o: after(x, rotated) for o, x in held.items()}
    for bit in bits[1:]:
        held.update({o ^ 1 << bit: partner(x, bit) for o, x in list(held.items())})
    grad_rows = arrange_rows(held, group_index, table)
    level(both, (backward, 0))
    for _ in range(4, last):
        level(both)
    sum_a = Scatter(ring, send, 1, partials[0])
    level([(ring_b, 1), (ring_a, -1), (sum_a, 1), (ring_b, -1)], (backward, 1))
    sum_b = Scatter(ring, send, -1, partials[1])
    level([(ring_b, 1), (sum_a, -1), (sum_a, 1), (sum_b, -1)], (forward, (0, 1)))
    both = [(sum_a, 1), (sum_a, -1), (sum_b, 1), (sum_b, -1)]
    level(both, (forward, (2,)))
    layer_output = running[-1]
    def halved(value, bit, *tokens):
        kept = value.shape[0] // 2
        other = partner(after(lax.slice_in_dim(value, kept, 2 * kept, axis=0), *tokens), bit)
        own = lax.slice_in_dim(value, 0, kept, axis=0)
        return (own.astype(F32) + other.astype(F32)).astype(BF16)

    before = [*done["hops"], *done["work"]]
    for bit in reversed(bits[1:]):
        layer_output = halved(layer_output, bit, *before)
    done["hops"].append(layer_output)
    level(both, (backward, 2))
    for _ in range(4, last):
        level(both)
    small_sum = Scatter(ring, send, 1, partials[2])

    small_both = [(small_sum, 1), (small_sum, -1)]
    level([(small_sum, 1), (sum_b, 1), (sum_b, -1)])
    first = exchanged(sum_a.total(partials[2]), [])
    layer_output = halved(layer_output, bits[0], first[2])
    for _ in range(2, last):
        level(small_both)
    total = sum_b.total()
    second = exchanged(total, [layer_output])
    level(small_both, None, total)
    grads = []
    for k, (start, size) in enumerate(back_streams):
        own, other, _ = (
            (first, second)[k] if k < 2 else exchanged(small_sum.total(), [second[2]], grads)
        )
        grads = local_grads(
            own, other, last_sign, mix, scale, gate_act, up_act, start, grads
        )
    gate_grad, up_grad = grads
    return (layer_output, gate_grad, up_grad)


def solution(mesh):
    return jax.shard_map(
        on_device,
        mesh=mesh,
        in_specs=(
            P("dp", "tensor"),
            P("dp", "tensor"),
            P("tensor", "dp"),
            P("tensor", "dp"),
            P("tensor", "dp"),
        ),
        out_specs=(P("tensor", "dp"), P("dp", "tensor"), P("dp", "tensor")),
        check_vma=False,
    )
```

```python
import math

import jax
import jax.numpy as jnp
import numpy as np
from jax import lax
from jax.experimental import pallas as pl
from jax.experimental.pallas import tpu as pltpu
from jax.sharding import PartitionSpec as P

BLOCK = 128
AHEAD = (5, 10, 11)
BACK = (11, 11, 4)
VMEM_LIMIT = 40 * 1024 * 1024
SUM_LIMIT = 52 * 1024 * 1024
F32, BF16 = jnp.float32, jnp.bfloat16


def after(value, *earlier):
    return lax.optimization_barrier((value, *earlier))[0]


def sylvester(order):
    matrix = np.ones((1, 1), np.float32)
    while matrix.shape[0] < order:
        matrix = np.block([[matrix, matrix], [matrix, -matrix]])
    return matrix


def ring_cycle(count):
    return [*range(0, count, 2), *reversed(range(1, count, 2))]


def ring_tables(count):
    cycle = ring_cycle(count)
    place = np.argsort(cycle)
    behind = [[cycle[(place[i] - r) % count] for r in range(count)] for i in range(count)]
    ahead = [[(place[j] - place[i]) % count for j in range(count)] for i in range(count)]
    return np.concatenate([behind, ahead], axis=1).astype(np.int32)


def params(limit=VMEM_LIMIT):
    return pltpu.CompilerParams(vmem_limit_bytes=limit)


def cost(operations, moved):
    return pl.CostEstimate(
        flops=operations // 16, bytes_accessed=moved // 16, transcendentals=0
    )


def spec_smem():
    return pl.BlockSpec(memory_space=pltpu.SMEM)


def dequantize_into(weight_ref, codes_ref, scales_ref, row0, col0):
    for i in range(codes_ref.shape[0] // BLOCK):
        for j in range(codes_ref.shape[1] // BLOCK):
            at = (pl.ds(i * BLOCK, BLOCK), pl.ds(j * BLOCK, BLOCK))
            wide = codes_ref[at].astype(F32) * scales_ref[row0 + i, col0 + j]
            weight_ref[at] = wide.astype(BF16)


def mixed(values, mix, scale):
    high = values.astype(BF16)
    low = (values - high.astype(F32)).astype(BF16)
    total = jnp.dot(high, mix, preferred_element_type=F32) + jnp.dot(
        low, mix, preferred_element_type=F32
    )
    return (total * scale).astype(BF16)


def mix_kernel(scale, sign_ref, mix_ref, own_ref, other_ref, out_ref):
    for j in range(own_ref.shape[1] // BLOCK):
        at = (slice(None), pl.ds(j * BLOCK, BLOCK))
        values = own_ref[at].astype(F32) * sign_ref[0] + other_ref[at].astype(F32)
        out_ref[at] = mixed(values, mix_ref[...], scale)


def local_mix(own, other, sign, mix, scale):
    rows, cols = own.shape
    return pl.pallas_call(
        lambda *refs: mix_kernel(scale, *refs),
        out_shape=jax.ShapeDtypeStruct((rows, cols), BF16),
        in_specs=[spec_smem()] + [pl.BlockSpec(memory_space=pltpu.VMEM)] * 3,
        out_specs=pl.BlockSpec(memory_space=pltpu.VMEM),
        compiler_params=params(),
        cost_estimate=cost(4 * rows * cols * BLOCK, 6 * rows * cols),
        name="local_mix",
    )(sign, mix, own, other)


def grads_kernel(scale, tile, sign_ref, mix_ref, own_ref, other_ref, gate_ref, up_ref, *refs):
    gate_grad_ref, up_grad_ref = refs[-2:]
    for j in range(tile // BLOCK):
        at = (slice(None), pl.ds(j * BLOCK, BLOCK))
        values = own_ref[at].astype(F32) * sign_ref[0] + other_ref[at].astype(F32)
        grad = mixed(values, mix_ref[...], scale).astype(F32)
        gate = gate_ref[at].astype(F32)
        sigmoid = jax.nn.sigmoid(gate)
        up_grad_ref[at] = (grad * (gate * sigmoid)).astype(BF16)
        gate_grad_ref[at] = (
            grad * up_ref[at].astype(F32) * sigmoid * (1.0 + gate * (1.0 - sigmoid))
        ).astype(BF16)


def local_grads(own, other, sign, mix, scale, gate_act, up_act, start, made):
    rows, cols = own.shape
    tile = math.gcd(start, cols)
    if tile % (2 * BLOCK) == 0:
        tile //= 2
    whole = pl.BlockSpec((rows, tile), lambda i: (0, start // tile + i))
    part = pl.BlockSpec((rows, tile), lambda i: (0, i))
    rest = [pl.BlockSpec(memory_space=pl.ANY)] * len(made)
    return pl.pallas_call(
        lambda *refs: grads_kernel(scale, tile, *refs),
        grid=(cols // tile,),
        out_shape=[jax.ShapeDtypeStruct(gate_act.shape, BF16)] * 2,
        in_specs=[
            spec_smem(),
            pl.BlockSpec((BLOCK, BLOCK), lambda i: (0, 0)),
            part,
            part,
            whole,
            whole,
            *rest,
        ],
        out_specs=[whole, whole],
        input_output_aliases={6 + k: k for k in range(len(made))},
        compiler_params=params(),
        cost_estimate=cost(4 * rows * cols * BLOCK, 12 * rows * cols),
        name="local_grads",
    )(sign, mix, own, other, gate_act, up_act, *made)


def arrange_kernel(count, group_ref, table_ref, *refs):
    out_ref = refs[-1]
    rows = out_ref.shape[0] // count
    for offset, block in enumerate(refs[:-1]):
        per = block.shape[0] // rows
        for i in range(per):
            place = table_ref[count + (group_ref[0] ^ offset) * per + i]
            start = pl.multiple_of(place * rows, rows)
            out_ref[pl.ds(start, rows), :] = block[pl.ds(i * rows, rows), :]


def arrange_rows(held, group, table):
    blocks = [held[offset] for offset in range(len(held))]
    rows, cols = blocks[0].shape
    return pl.pallas_call(
        lambda *refs: arrange_kernel(table.shape[0] // 2, *refs),
        out_shape=jax.ShapeDtypeStruct((rows * len(blocks), cols), BF16),
        in_specs=[spec_smem()] * 2 + [pl.BlockSpec(memory_space=pltpu.VMEM)] * len(blocks),
        out_specs=pl.BlockSpec(memory_space=pltpu.VMEM),
        compiler_params=params(),
        cost_estimate=cost(0, 4 * rows * cols * len(blocks)),
        name="arrange_rows",
    )(group, table, *blocks)


def backward_kernel(row_block, scales_ref, grad_ref, codes_ref, out_ref, weight_ref):
    row0 = row_block + pl.program_id(0) * (codes_ref.shape[0] // BLOCK)
    dequantize_into(weight_ref, codes_ref, scales_ref, row0, 0)
    out_ref[...] = lax.dot_general(
        grad_ref[...], weight_ref[...], (((1,), (1,)), ((), ())), preferred_element_type=F32
    ).astype(BF16)


def backward_product(grad_rows, codes, scales, start, cols, tile):
    tokens, depth = grad_rows.shape
    if start % (2 * tile) == 0 and cols % (2 * tile) == 0:
        tile *= 2
    return pl.pallas_call(
        lambda *refs: backward_kernel(start // BLOCK, *refs),
        grid=(cols // tile,),
        out_shape=pltpu.HBM((tokens, cols), BF16),
        in_specs=[
            spec_smem(),
            pl.BlockSpec((tokens, depth), lambda i: (0, 0)),
            pl.BlockSpec((tile, depth), lambda i: (start // tile + i, 0)),
        ],
        out_specs=pl.BlockSpec((tokens, tile), lambda i: (0, i)),
        scratch_shapes=[pltpu.VMEM((tile, depth), BF16)],
        compiler_params=params(),
        cost_estimate=cost(
            2 * tokens * depth * cols, 2 * (tokens * depth + (depth + tokens) * cols)
        ),
        name="backward_product",
    )(scales, grad_rows, codes)


def forward_kernel(counts, bits, row_block, has_sum, group_ref, order_ref, scales_ref, *refs):
    total_blocks = sum(counts)
    blocks, codes_ref = refs[:total_blocks], refs[total_blocks]
    sum_ref = refs[total_blocks + 1] if has_sum else None
    out_ref, rows_ref, weight_ref, sems = refs[-4:]
    tile = codes_ref.shape[1]
    per = max(1, counts[0] >> bits)
    step = pl.program_id(0)

    def places():
        column = 0
        for part, count in enumerate(counts):
            for r in range(count):
                i = part * count + r
                size, width = blocks[i].shape
                offset = order_ref[r] // per ^ group_ref[0]
                turned = sum((offset >> k & 1) << bits - 1 - k for k in range(bits))
                start = pl.multiple_of((turned * per + order_ref[r] % per) * size, size)
                yield i, rows_ref.at[pl.ds(start, size), pl.ds(column, width)]
            column += blocks[part * count].shape[1]

    def copies():
        return [pltpu.make_async_copy(blocks[i], place, sems.at[i]) for i, place in places()]

    @pl.when(step == 0)
    def _():
        if len(counts) == 1:
            for i, place in places():
                place[...] = blocks[i][...]
        else:
            for copy in copies():
                copy.start()

    dequantize_into(weight_ref, codes_ref, scales_ref, row_block, step * (tile // BLOCK))

    if len(counts) > 1:

        @pl.when(step == 0)
        def _():
            for copy in copies():
                copy.wait()

    total = jnp.dot(rows_ref[...], weight_ref[...], preferred_element_type=F32)
    if has_sum:
        total = total + sum_ref[...]
    out_ref[...] = total.astype(out_ref.dtype)


def forward_product(parts, bits, group, order, codes, scales, start, running, out_dtype):
    size, count = parts[0][0].shape[0], len(parts[0])
    depth = sum(blocks[0].shape[1] for blocks in parts)
    tokens, width = size * count, codes.shape[1]
    tile = min(512 if len(parts) > 1 else 256, width)
    if len(parts) > 1:
        block = pl.BlockSpec(memory_space=pltpu.HBM)
    else:
        block = pl.BlockSpec((size, depth), lambda i: (0, 0), pipeline_mode=pl.Buffered(1))
    sums = [] if running is None else [running]
    sliced = pl.BlockSpec((tokens, tile), lambda i: (0, i))
    return pl.pallas_call(
        lambda *refs: forward_kernel(
            [count] * len(parts), bits, start // BLOCK, bool(sums), *refs
        ),
        grid=(width // tile,),
        out_shape=pltpu.HBM((tokens, width), out_dtype),
        in_specs=[
            spec_smem(),
            spec_smem(),
            spec_smem(),
            *[block] * (count * len(parts)),
            pl.BlockSpec((pl.Element(depth), pl.Element(tile)), lambda i: (start, i * tile)),
            *[sliced] * len(sums),
        ],
        out_specs=sliced,
        scratch_shapes=[
            pltpu.VMEM((tokens, depth), BF16),
            pltpu.VMEM((depth, tile), BF16),
            pltpu.SemaphoreType.DMA((count * len(parts),)),
        ],
        compiler_params=params(SUM_LIMIT if sums else VMEM_LIMIT),
        cost_estimate=cost(
            2 * tokens * depth * width, 2 * (tokens + width) * depth + 8 * tokens * width
        ),
        name="forward_product",
    )(group, order, scales, *[block for blocks in parts for block in blocks], codes, *sums)


def shares(units, parts):
    ends = [round(units * sum(parts[: i + 1]) / sum(parts)) for i in range(len(parts))]
    return [end - begin for begin, end in zip([0, *ends], ends)]


def stream_columns(sizes, tile):
    starts = np.cumsum([0, *sizes[:-1]])
    return [(int(a) * tile, int(b) * tile) for a, b in zip(starts, sizes)]


class Ring:
    def __init__(self, count, send, long_way):
        self.count, self.send = count, send
        self.reach = {long_way: count // 2, -long_way: count - 1 - count // 2}
        self.hops = {1: 0, -1: 0}

    def advance(self, step, *tokens):
        moving = self.outgoing(step)
        self.hops[step] += 1
        arrived = self.send(after(moving, *tokens), step)
        self.incoming(step, arrived)
        return arrived


class Gather(Ring):
    def __init__(self, count, send, long_way, own):
        super().__init__(count, send, long_way)
        self.blocks = {0: own}

    def outgoing(self, step):
        return self.blocks[self.hops[step] * step % self.count]

    def incoming(self, step, arrived):
        self.blocks[self.hops[step] * step % self.count] = arrived

    def all_blocks(self):
        return [self.blocks[r] for r in range(self.count)]


class Scatter(Ring):
    def __init__(self, count, send, long_way, terms):
        super().__init__(count, send, long_way)
        self.terms, self.sums = terms, {}

    def term(self, offset):
        rows = self.terms.shape[0] // self.count
        at = offset % self.count * rows
        return lax.slice_in_dim(self.terms, at, at + rows, axis=0)

    def outgoing(self, step):
        term = self.term(step * (self.reach[step] - self.hops[step]))
        if step not in self.sums:
            return term
        return (self.sums[step].astype(F32) + term.astype(F32)).astype(BF16)

    def incoming(self, step, arrived):
        self.sums[step] = arrived

    def total(self, *tokens):
        parts = [after(part, *tokens) for part in (self.term(0), *self.sums.values())]
        return sum(part.astype(F32) for part in parts).astype(BF16)


def on_device(gate_act, up_act, down_codes, down_scales, grad_out):
    groups, ring = lax.axis_size("tensor"), lax.axis_size("dp")
    group, member = lax.axis_index("tensor"), lax.axis_index("dp")
    bits = list(reversed(range(groups.bit_length() - 1)))
    rows, hidden_units = gate_act.shape
    tile = 256 if hidden_units % 256 == 0 else BLOCK
    units = hidden_units // tile
    ahead_streams = stream_columns(shares(units, AHEAD), tile)
    back_streams = stream_columns(shares(units, BACK), tile)
    cycle = ring_cycle(ring)
    table = lax.dynamic_index_in_dim(jnp.asarray(ring_tables(ring)), member, 0, keepdims=False)

    def send(value, step):
        return lax.ppermute(
            value, "dp", [(cycle[i], cycle[(i + step) % ring]) for i in range(ring)]
        )

    def partner(value, bit):
        return lax.ppermute(value, "tensor", [(i, i ^ 1 << bit) for i in range(groups)])

    def sign(bit):
        return jnp.where(group >> bit & 1 == 1, -1.0, 1.0).astype(F32)

    def paired(own, other, bit):
        return (own.astype(F32) * sign(bit) + other.astype(F32)).astype(BF16)

    group_index = group.astype(jnp.int32).reshape(1)
    last_sign = sign(bits[-1]).reshape(1)
    mix = jnp.asarray(sylvester(BLOCK), BF16)
    scale = 1.0 / math.sqrt(groups * BLOCK)

    def hidden(start, size):
        gate = lax.slice_in_dim(gate_act, start, start + size, axis=1).astype(F32)
        up = lax.slice_in_dim(up_act, start, start + size, axis=1).astype(F32)
        return (gate * jax.nn.sigmoid(gate) * up).astype(BF16)

    def exchanged(own, token, later=()):
        own = after(own, *token)
        other = arrived = partner(own, bits[0])
        other = after(other, *later)
        for previous, bit in zip(bits, bits[1:]):
            own = paired(own, other, previous)
            other = partner(own, bit)
        return own, other, arrived

    last = ring // 2
    gathers, token, seen, later = [], [], [], []
    for k, (start, size) in enumerate(ahead_streams):
        if k == 1:
            later = hop
        if k == 2:
            for _ in range(3, last):
                later = [gathers[0].advance(step, rotated) for step in (1, -1)]
            later += [gathers[0].advance(1)]
        own, other, arrived = exchanged(hidden(start, size), token, later)
        if k == 1:
            seen = [gathers[0].advance(step) for step in (1, -1)]
        if k == 2:
            seen = hop
        rotated = local_mix(own, after(other, *seen), last_sign, mix, scale)
        gathers.append(Gather(ring, send, -1 if k == 1 else 1, rotated))
        token = [arrived]
        if k < 2:
            hop = [gathers[k].advance(step) for step in (1, -1)]
        if k == 1:
            token += seen
    own = after(grad_out, *token)
    held = {0: own, 1 << bits[0]: partner(own, bits[0])}
    _, ring_a, ring_b = gathers

    running, partials = [None], []

    def forward(which, *tokens):
        running.append(
            forward_product(
                [gathers[k].all_blocks() for k in which],
                len(bits),
                group_index,
                after(table, *tokens),
                down_codes,
                down_scales,
                ahead_streams[which[0]][0],
                running[-1],
                BF16 if which[-1] == len(gathers) - 1 else F32,
            )
        )
        return running[-1]

    def backward(k, *tokens):
        start, cols = back_streams[k]
        partials.append(
            backward_product(after(grad_rows, *tokens), down_codes, down_scales, start, cols, tile)
        )
        return partials[-1]

    done = {"hops": [*hop, rotated], "work": []}

    def level(hops, work=None, *tokens):
        before = [*done["hops"], *done["work"]]
        done["hops"] = [current.advance(step, *done["work"], *tokens) for current, step in hops]
        done["work"] = [work[0](*work[1:], *before)] if work else []

    both = [(ring_a, -1), (ring_b, 1), (ring_a, 1), (ring_b, -1)]
    level(both)
    held = {o: after(x, rotated) for o, x in held.items()}
    for bit in bits[1:]:
        held.update({o ^ 1 << bit: partner(x, bit) for o, x in list(held.items())})
    grad_rows = arrange_rows(held, group_index, table)
    level(both, (backward, 0))
    for _ in range(4, last):
        level(both)
    sum_a = Scatter(ring, send, 1, partials[0])
    level([(ring_b, 1), (ring_a, -1), (sum_a, 1), (ring_b, -1)], (backward, 1))
    sum_b = Scatter(ring, send, -1, partials[1])
    level([(ring_b, 1), (sum_a, -1), (sum_a, 1), (sum_b, -1)], (forward, (0, 1)))
    both = [(sum_a, 1), (sum_a, -1), (sum_b, 1), (sum_b, -1)]
    level(both, (forward, (2,)))
    layer_output = running[-1]
    def halved(value, bit, *tokens):
        kept = value.shape[0] // 2
        other = partner(after(lax.slice_in_dim(value, kept, 2 * kept, axis=0), *tokens), bit)
        own = lax.slice_in_dim(value, 0, kept, axis=0)
        return (own.astype(F32) + other.astype(F32)).astype(BF16)

    before = [*done["hops"], *done["work"]]
    for bit in reversed(bits[1:]):
        layer_output = halved(layer_output, bit, *before)
    done["hops"].append(layer_output)
    level(both, (backward, 2))
    for _ in range(4, last):
        level(both)
    small_sum = Scatter(ring, send, 1, partials[2])

    small_both = [(small_sum, 1), (small_sum, -1)]
    level([(small_sum, 1), (sum_b, 1), (sum_b, -1)])
    first = exchanged(sum_a.total(partials[2]), [])
    layer_output = halved(layer_output, bits[0], first[2])
    for _ in range(2, last):
        level(small_both)
    total = sum_b.total()
    second = exchanged(total, [layer_output])
    level(small_both, None, total)
    grads = []
    for k, (start, size) in enumerate(back_streams):
        own, other, _ = (
            (first, second)[k] if k < 2 else exchanged(small_sum.total(), [second[2]], grads)
        )
        grads = local_grads(
            own, other, last_sign, mix, scale, gate_act, up_act, start, grads
        )
    gate_grad, up_grad = grads
    return (layer_output, gate_grad, up_grad)


def solution(mesh):
    return jax.shard_map(
        on_device,
        mesh=mesh,
        in_specs=(
            P("dp", "tensor"),
            P("dp", "tensor"),
            P("tensor", "dp"),
            P("tensor", "dp"),
            P("tensor", "dp"),
        ),
        out_specs=(P("tensor", "dp"), P("dp", "tensor"), P("dp", "tensor")),
        check_vma=False,
    )
```
